128 devices in a mesh: ctx: 16 (over x, y), exp: 8 (over z, core).
Axes of the slice: x: 4, y: 4, z: 4, core: 2. Of those that a mesh axis runs over, the one named last changes fastest.
Arguments:
- queries: bfloat16 [1024, 8192], P('ctx', 'exp'), may hold values from -6 to 6
- key_rows: bfloat16 [1024, 1024], P('ctx', 'exp'), may hold values from -8 to 8
- values: bfloat16 [1024, 1024], P('ctx', 'exp'), may hold values from -6 to 6
- span_order: int32 [16], replicated, may hold values from 0 to 15, each once
- residual: bfloat16 [1024, 4096], P(('ctx', 'exp')), may hold values from -3 to 3
- out_weight: bfloat16 [8192, 4096], P('exp', 'ctx'), may hold values from -0.0625 to 0.0625
- norm_gain: bfloat16 [4096], replicated, may hold values from 0.099609375 to 1.8984375
- routes: int32 [1024, 2], P(('ctx', 'exp')), may hold values from 0 to 7, all different within a row; in each aligned block of 8 rows (0 to 7, 8 to 15, ...) at most 4 rows name the same one
- route_gates: float32 [1024, 2], P(('ctx', 'exp')), may hold values from 0.2 to 1
- gate_proj: bfloat16 [8, 4096, 12288], P('exp', None, 'ctx'), may hold values from -0.09375 to 0.09375
- up_proj: bfloat16 [8, 4096, 12288], P('exp', None, 'ctx'), may hold values from -0.09375 to 0.09375
- down_proj: bfloat16 [8, 12288, 4096], P('exp', 'ctx'), may hold values from -0.0546875 to 0.0546875
Outputs:
- layer_out: bfloat16 [1024, 4096], P(('ctx', 'exp'))
The draws below stay inside these ranges and needn't reach their ends.
Inputs may be any that keep to these rules, and one draw needn't show every extreme that they name: `routes`: each row names two different experts; among the 8 rows of one device no expert is named more than 4 times, and in some devices' rows one expert is named exactly 4 times. `span_order`: a permutation of the block numbers.
All inputs are finite; a program needn't handle non-finite values.
Results may differ from the reference program's by a relative error of at most 0.024.
Values may be sent and summed in bfloat16 or wider, within the bound.
No kernel may reach another device: no remote copies, remote signals or barrier semaphores. Data moves between devices by JAX's collectives and lax.ppermute only.
A program may use at most 128 MiB of HBM per device.

```python
import math
import jax
import jax.numpy as jnp
import numpy as np
from jax import lax

D = 4096
FF = 12288
HEADS = 64
KV_HEADS = 8
HD = 128
CYCLE_STEPS = 4
TOK_MOE = 8
CAP = 4
BLK = 64
TOKENS = 1024
EXPERTS = 8
N_CTX = 16
N_EXP = 8


def draw_key_rows(key, part):
    key = jax.random.fold_in(key, 3)
    base = jnp.clip(jax.random.normal(key, (TOKENS, KV_HEADS * HD), jnp.float32), -6.0, 6.0)
    return base.astype(jnp.bfloat16)


def draw_queries(key, part):
    key = jax.random.fold_in(key, 5)
    base = jnp.clip(jax.random.normal(key, (TOKENS, HEADS * HD), jnp.float32), -6.0, 6.0)
    return base.astype(jnp.bfloat16)


def shard_levels(own_key, extent, pieces, least, top_value):
    factor_of = 1.0
    for position, blocks in pieces:
        draws = jax.random.uniform(jax.random.fold_in(jax.random.fold_in(own_key, 6), position), (blocks,), jnp.float32, least / len(pieces), top_value / len(pieces))
        factor_of = factor_of * jnp.repeat(jnp.exp(draws), extent[position] // blocks).reshape((-1,) + (1,) * (len(extent) - 1 - position))
    return factor_of


def deal_out(rng, own, number, rows, amount, top, limit, slope):
    sequence = jax.random.permutation(rng, amount)
    heavy_load, ordinary = load_shares(amount, rows * top, limit, slope, True), load_shares(amount, rows * top, limit, slope, False)
    places = jnp.arange(amount)

    def named(lengths, rotation):
        used = int((lengths > 0).sum())
        fixed = max(1, used // 4)
        shifted = fixed + (places - fixed + rotation * (used - fixed)) % max(1, amount - fixed)
        return jnp.zeros((amount,), jnp.int32).at[sequence[jnp.where(places < fixed, places, shifted)]].set(jnp.asarray(lengths, jnp.int32))

    lengths = jnp.where(number % 4 == 0, named(heavy_load, number // 4), named(ordinary, number - number // 4 - 1))
    mixed = jax.random.permutation(jax.random.fold_in(own, 3), amount)
    source_of, taker = mixed[0:amount // 2 * 2:2], mixed[1:amount // 2 * 2:2]
    room = jnp.minimum(lengths[source_of] - 1, limit - lengths[taker]) // 2
    room = jnp.where((source_of == sequence[0]) | (taker == sequence[0]) | (lengths[taker] == 0), 0, jnp.maximum(room, 0))
    shifted = jax.random.randint(jax.random.fold_in(own, 4), (amount // 2,), 0, 1 << 20) % (room + 1)
    lengths = lengths.at[source_of].add(-shifted).at[taker].add(shifted)
    members = jnp.searchsorted(jnp.cumsum(lengths), jnp.arange(rows * top), side="right").astype(jnp.int32)
    table = members.reshape(top, rows).T
    table = table[jax.random.permutation(jax.random.fold_in(own, 1), rows)]
    rotation = jax.random.randint(jax.random.fold_in(own, 2), (rows, 1), 0, top)
    return jnp.take_along_axis(table, (jnp.arange(top)[None, :] + rotation) % top, axis=1)


def load_shares(amount, total, limit, slope, full):
    portions = [(1 << 20) // math.isqrt(grade ** slope) + 1 for grade in range(1, amount + 1)]
    largest = limit if full else min(limit, max(-(-total // amount), total * portions[0] // sum(portions)))
    least = 1 if total - largest >= amount - 1 else 0
    given, spare = [largest] + [least] * (amount - 1), total - largest - least * (amount - 1)
    while spare > 0:
        movable = [i for i in range(1, amount) if given[i] < largest] or [i for i in range(1, amount) if given[i] < limit]
        whole, remaining = sum([portions[i] for i in movable]), spare
        for i in movable:
            addition = min(limit - given[i], max(1, remaining * portions[i] // whole), spare)
            given[i] = given[i] + addition
            spare = spare - addition
    return np.array(given)


def gaussian(rng, shape, deviation, most, pieces=(), held_as=jnp.bfloat16):
    entries = deviation * jax.random.normal(rng, shape, jnp.float32)
    if pieces:
        entries = entries * shard_levels(rng, shape, pieces, -0.22, 0.18)
    return jnp.clip(entries, -most, most).astype(held_as)


def setup_inputs(seed: int = 0) -> dict:
    key_of = jax.random.split(jax.random.key(seed), 13)
    queries = draw_queries(jax.random.fold_in(key_of[12], 71), 0)
    key_rows = draw_key_rows(jax.random.fold_in(key_of[12], 71), 0)
    values = gaussian(key_of[2], (TOKENS, KV_HEADS * HD), 1.0, 6.0, ((0, 16), (1, 8)))
    span_order = jax.random.permutation(key_of[3], N_CTX).astype(jnp.int32)
    residual = gaussian(key_of[4], (TOKENS, D), 0.5, 3.0, ((0, 128),))
    out_weight = gaussian(key_of[5], (HEADS * HD, D), (HEADS * HD) ** -0.5, 0.0625, ((0, 8), (1, 16)))
    norm_gain = jnp.clip(1.0 + 0.18 * jax.random.normal(key_of[6], (D,), jnp.float32), 0.099609375, 1.8984375).astype(jnp.bfloat16)
    routes_keys = jax.random.split(jax.random.fold_in(key_of[7], 1), TOKENS // TOK_MOE)
    routes_turns = jax.random.permutation(jax.random.fold_in(key_of[7], 3), TOKENS // TOK_MOE)
    routes = jax.vmap(lambda own, number: deal_out(jax.random.fold_in(key_of[7], 2), own, number, TOK_MOE, EXPERTS, 2, CAP, 2))(routes_keys, routes_turns).reshape((TOKENS, 2))
    route_gates = jnp.clip(0.2 + 0.8 * jax.random.uniform(key_of[8], (TOKENS, 2), jnp.float32) ** shard_levels(key_of[8], (TOKENS, 2), ((0, 128),), -0.2, 0.2), 0.2, 1.0)
    gate_proj = gaussian(key_of[9], (EXPERTS, D, FF), D ** -0.5, 0.09375, ((0, 8), (2, 16)))
    up_proj = gaussian(key_of[10], (EXPERTS, D, FF), D ** -0.5, 0.09375, ((0, 8), (2, 16)))
    down_proj = gaussian(key_of[11], (EXPERTS, FF, D), FF ** -0.5, 0.0546875, ((0, 8), (1, 16)))
    return dict(queries=queries, key_rows=key_rows, values=values, span_order=span_order, residual=residual, out_weight=out_weight, norm_gain=norm_gain, routes=routes, route_gates=route_gates, gate_proj=gate_proj, up_proj=up_proj, down_proj=down_proj)


def reference(queries, key_rows, values, span_order, residual, out_weight, norm_gain, routes, route_gates, gate_proj, up_proj, down_proj):
    group = HEADS // KV_HEADS
    scale = 1.0 / math.sqrt(HD)
    query_blocks = queries.reshape(N_CTX, BLK, KV_HEADS, group, HD)
    key_blocks = key_rows.reshape(N_CTX, BLK, KV_HEADS, HD)
    value_blocks = values.reshape(N_CTX, BLK, KV_HEADS, HD)
    offsets = jnp.arange(BLK, dtype=jnp.int32)

    def one_block(block):
        query_here = query_blocks[block].astype(jnp.float32)
        query_pos = span_order[block] * BLK + offsets
        sources = [(block - step) % N_CTX for step in range(CYCLE_STEPS)]
        keys_here = jnp.concatenate([key_blocks[source] for source in sources], axis=0).astype(jnp.float32)
        values_here = jnp.concatenate([value_blocks[source] for source in sources], axis=0).astype(jnp.float32)
        key_pos = jnp.concatenate([span_order[source] * BLK + offsets for source in sources])
        scores = jnp.einsum('qkgd,lkd->kgql', query_here, keys_here) * scale
        admitted = key_pos[None, :] <= query_pos[:, None]
        scores = jnp.where(admitted[None, None], scores, -1e+30)
        row_max = lax.optimization_barrier(jnp.max(scores, axis=-1, keepdims=True))
        exp_scores = jnp.exp(scores - row_max)
        attend_probs = (exp_scores / lax.optimization_barrier(jnp.sum(exp_scores, axis=-1, keepdims=True))).astype(jnp.bfloat16)
        mixed = jnp.einsum('kgql,lkd->qkgd', attend_probs.astype(jnp.float32), values_here)
        return mixed.astype(jnp.bfloat16).reshape(BLK, HEADS * HD)
    attended = lax.map(one_block, jnp.arange(N_CTX, dtype=jnp.int32)).reshape(N_CTX * BLK, HEADS * HD)
    projected = jnp.dot(attended, out_weight, preferred_element_type=jnp.float32)
    hidden_state = (residual.astype(jnp.float32) + projected).astype(jnp.bfloat16)
    hidden_wide = hidden_state.astype(jnp.float32)
    inverse = lax.rsqrt(lax.optimization_barrier(jnp.mean(hidden_wide * hidden_wide, axis=-1, keepdims=True)) + 1e-06)
    normed = (hidden_wide * inverse * norm_gain.astype(jnp.float32)).astype(jnp.bfloat16)
    flat_routes = routes.reshape(-1)
    pair_count = flat_routes.shape[0]
    bound = N_CTX * N_EXP * CAP

    def one_expert(expert):
        picked = jnp.nonzero(flat_routes == expert, size=bound, fill_value=pair_count)[0].astype(jnp.int32)
        token_index = jnp.minimum(picked // 2, pair_count // 2 - 1).astype(jnp.int32)
        token_rows = normed[token_index]
        gate_act = jnp.dot(token_rows, gate_proj[expert], preferred_element_type=jnp.float32)
        up_act = jnp.dot(token_rows, up_proj[expert], preferred_element_type=jnp.float32)
        inner = (jax.nn.silu(gate_act) * up_act).astype(jnp.bfloat16)
        result = jnp.dot(inner, down_proj[expert], preferred_element_type=jnp.float32).astype(jnp.bfloat16)
        return (picked, result)
    picked_all, results = lax.map(one_expert, jnp.arange(EXPERTS, dtype=jnp.int32))
    pair_out = jnp.zeros((pair_count, D), jnp.bfloat16)
    pair_out = pair_out.at[picked_all.reshape(-1)].set(results.reshape(-1, D), mode='drop')
    pair_out = pair_out.reshape(pair_count // 2, 2, D).astype(jnp.float32)
    gates = route_gates.astype(jnp.float32)
    total = hidden_wide + gates[:, 0:1] * pair_out[:, 0] + gates[:, 1:2] * pair_out[:, 1]
    return total.astype(jnp.bfloat16)
```

```python
import math

import jax
import jax.numpy as jnp
from jax import lax
from jax.experimental import pallas as pl
from jax.experimental.pallas import tpu as pltpu
from jax.sharding import PartitionSpec as P

HEADS = 64
KV_HEADS = 8
HD = 128
CYCLE_STEPS = 4
CAP = 4
SIDE = 4
BOTH = ("ctx", "exp")
SHIFTS = (1, 3, 2)


def number(x, y, z, core):
    return (((x % SIDE) * SIDE + y % SIDE) * SIDE + z % SIDE) * 2 + core


def everyone():
    return [
        (x, y, z, core)
        for x in range(SIDE)
        for y in range(SIDE)
        for z in range(SIDE)
        for core in range(2)
    ]


def first_axis(d):
    return [
        (number(x, y, z, c), number(x + d * c, y + d * (1 - c), z, c)) for x, y, z, c in everyone()
    ]


def second_axis(d):
    return [
        (number(x, y, z, c), number(x + d * (1 - c), y + d * c, z, c)) for x, y, z, c in everyone()
    ]


def z_axis(d):
    return [(number(x, y, z, c), number(x, y, z + d, c)) for x, y, z, c in everyone()]


def sibling(shard):
    pairs = [(number(x, y, z, c), number(x, y, z, 1 - c)) for x, y, z, c in everyone()]
    return lax.ppermute(shard, BOTH, pairs)


def gathered(shard, along):
    got = {0: shard}
    for d in SHIFTS:
        got[d] = lax.ppermute(shard, BOTH, along(d))
    return [got[d] for d in range(SIDE)]


def dealt(blocks, along, sign):
    got = {0: blocks[0]}
    for d in SHIFTS:
        got[d] = lax.ppermute(blocks[d], BOTH, along(sign * d))
    return [got[d] for d in range(SIDE)]


def added(blocks):
    total = blocks[0].astype(jnp.float32)
    for block in blocks[1:]:
        total = total + block.astype(jnp.float32)
    return total


def expert_kernel(x_ref, gate_ref, up_ref, down_ref, out_ref, acc_ref):
    step = pl.program_id(0)
    x = x_ref[...]
    gate = jnp.dot(x, gate_ref[...], preferred_element_type=jnp.float32)
    up = jnp.dot(x, up_ref[...], preferred_element_type=jnp.float32)
    inner = (gate / (1.0 + jnp.exp(-gate)) * up).astype(jnp.bfloat16)
    part = jnp.dot(inner, down_ref[...], preferred_element_type=jnp.float32)

    @pl.when(step == 0)
    def _():
        acc_ref[...] = part

    @pl.when(jnp.logical_and(step > 0, step < pl.num_programs(0) - 1))
    def _():
        acc_ref[...] += part

    @pl.when(step == pl.num_programs(0) - 1)
    def _():
        out_ref[...] = (acc_ref[...] + part).astype(out_ref.dtype)


def expert(x, gate, up, down):
    rows, width = x.shape
    hidden = gate.shape[1]
    tile = 256
    steps = hidden // tile
    return pl.pallas_call(
        expert_kernel,
        grid=(steps,),
        in_specs=[
            pl.BlockSpec((rows, width), lambda j: (0, 0)),
            pl.BlockSpec((width, tile), lambda j: (0, j)),
            pl.BlockSpec((width, tile), lambda j: (0, j)),
            pl.BlockSpec((tile, width), lambda j: (j, 0)),
        ],
        out_specs=pl.BlockSpec((rows, width), lambda j: (0, 0)),
        out_shape=jax.ShapeDtypeStruct((rows, width), jnp.bfloat16),
        scratch_shapes=[pltpu.VMEM((rows, width), jnp.float32)],
        compiler_params=pltpu.CompilerParams(vmem_limit_bytes=56 * 1024 * 1024),
        cost_estimate=pl.CostEstimate(
            flops=6 * rows * width * hidden,
            bytes_accessed=6 * width * hidden + 4 * rows * width,
            transcendentals=rows * hidden,
        ),
    )(x, gate, up, down)


def per_device(
    queries,
    key_rows,
    values,
    span_order,
    residual,
    out_weight,
    norm_gain,
    routes,
    route_gates,
    gate_proj,
    up_proj,
    down_proj,
):
    n_ctx = lax.axis_size("ctx")
    n_exp = lax.axis_size("exp")
    here = lax.axis_index("ctx")
    column = lax.axis_index("exp")
    core = column % 2
    z_here = column // 2
    block_rows = queries.shape[0]
    group = HEADS // KV_HEADS
    kv_local = key_rows.shape[1] // HD
    width = kv_local * HD
    token_count, model = residual.shape
    offsets = jnp.arange(block_rows, dtype=jnp.int32)
    query_pos = span_order[here] * block_rows + offsets

    packed = jnp.concatenate([key_rows, values], axis=1)
    collected = [packed]
    positions = [query_pos]
    for step in range(1, CYCLE_STEPS):
        pairs = [(i, (i + step) % n_ctx) for i in range(n_ctx)]
        collected.append(lax.ppermute(packed, "ctx", pairs))
        positions.append(span_order[(here - step) % n_ctx] * block_rows + offsets)
    weight_other = sibling(out_weight)
    stacked = jnp.concatenate(collected, axis=0)
    key_all = stacked[:, :width].reshape(-1, kv_local, HD)
    value_all = stacked[:, width:].reshape(-1, kv_local, HD)
    key_pos = jnp.concatenate(positions)
    query_heads = queries.reshape(block_rows, kv_local, group, HD)
    scores = jnp.einsum(
        "qkgd,lkd->kgql", query_heads, key_all, preferred_element_type=jnp.float32
    ) * (1.0 / math.sqrt(HD))
    admitted = key_pos[None, :] <= query_pos[:, None]
    scores = jnp.where(admitted[None, None], scores, -1e30)
    row_max = jnp.max(scores, axis=-1, keepdims=True)
    exp_scores = jnp.exp(scores - row_max)
    attend_probs = (exp_scores / jnp.sum(exp_scores, axis=-1, keepdims=True)).astype(jnp.bfloat16)
    mixed = jnp.einsum(
        "kgql,lkd->qkgd", attend_probs, value_all, preferred_element_type=jnp.float32
    )
    attended = mixed.astype(jnp.bfloat16).reshape(SIDE, 2, token_count, kv_local * group * HD)

    half = SIDE * token_count
    rows_0 = attended[:, 0].reshape(half, -1)
    rows_1 = attended[:, 1].reshape(half, -1)
    kept = jnp.where(core == 0, rows_0, rows_1)
    given = jnp.where(core == 0, rows_1, rows_0)
    paired = jnp.concatenate([kept, sibling(given)], axis=1)
    weight = jnp.concatenate([out_weight, weight_other], axis=0)
    line = jnp.concatenate(gathered(paired, first_axis), axis=0)
    plane = jnp.concatenate(gathered(line, second_axis), axis=0)
    partial_value = jnp.dot(plane, weight, preferred_element_type=jnp.float32)
    columns = partial_value.shape[1]
    partial_value = partial_value.reshape(n_ctx, SIDE, token_count, columns)
    by_z = jnp.roll(jnp.moveaxis(partial_value, 1, 0), -z_here, axis=0)
    others = dealt([by_z[0]] + [by_z[d].astype(jnp.bfloat16) for d in range(1, SIDE)], z_axis, 1)
    slab = added(others).astype(jnp.bfloat16)
    x_here, y_here = here // SIDE, here % SIDE
    target = jnp.arange(n_ctx, dtype=jnp.int32)
    back_x = (x_here - target // SIDE) % SIDE
    back_y = (y_here - target % SIDE) % SIDE
    place = jnp.where(core == 0, back_x * SIDE + back_y, back_y * SIDE + back_x)
    slab = jnp.take(slab, place, axis=0)
    owned = lax.all_to_all(slab, "ctx", split_axis=0, concat_axis=0, tiled=True)
    projected = jnp.moveaxis(owned, 0, 1).reshape(token_count, model).astype(jnp.float32)
    hidden_wide = (
        (residual.astype(jnp.float32) + projected).astype(jnp.bfloat16).astype(jnp.float32)
    )
    inverse = lax.rsqrt(jnp.mean(hidden_wide * hidden_wide, axis=-1, keepdims=True) + 1e-06)
    normed = (hidden_wide * inverse * norm_gain.astype(jnp.float32)).astype(jnp.bfloat16)

    slots = n_exp * CAP
    flat_routes = routes.reshape(-1)
    pair_ids = jnp.arange(flat_routes.shape[0], dtype=jnp.int32)
    same_expert = flat_routes[:, None] == flat_routes[None, :]
    earlier = pair_ids[None, :] < pair_ids[:, None]
    slot_number = jnp.sum(jnp.where(same_expert & earlier, 1, 0), axis=1).astype(jnp.int32)
    ahead = (flat_routes // 2 - z_here) % SIDE
    target = (ahead * 2 + (flat_routes + core) % 2) * CAP + slot_number
    match_table = jnp.where(
        target[:, None] == jnp.arange(slots, dtype=jnp.int32)[None, :], 1.0, 0.0
    ).astype(jnp.bfloat16)
    assign = match_table.reshape(token_count, 2, slots).sum(axis=1)
    send_rows = jnp.einsum("ts,td->sd", assign, normed, preferred_element_type=jnp.float32).astype(
        jnp.bfloat16
    )
    per_z = 2 * CAP
    sent = dealt([send_rows[d * per_z : (d + 1) * per_z] for d in range(SIDE)], z_axis, 1)
    column_rows = jnp.concatenate([r[:CAP] for r in sent] + [r[CAP:] for r in sent], axis=0)
    n1 = SIDE * CAP
    line = gathered(column_rows, first_axis)
    line = jnp.concatenate([r[:n1] for r in line] + [r[n1:] for r in line], axis=0)
    n2 = SIDE * n1
    plane = gathered(line, second_axis)
    mine = [r[:n2] for r in plane]
    theirs = sibling(jnp.concatenate([r[n2:] for r in plane], axis=0))
    rows_in = jnp.concatenate(mine + [theirs], axis=0)
    rows_out = expert(rows_in, gate_proj[0], up_proj[0], down_proj[0])
    n3 = SIDE * n2
    swapped = sibling(rows_out[n3:])
    plane = [
        jnp.concatenate([rows_out[d * n2 : (d + 1) * n2], swapped[d * n2 : (d + 1) * n2]], axis=0)
        for d in range(SIDE)
    ]
    line = added(dealt(plane, second_axis, -1)).astype(jnp.bfloat16)
    line = [
        jnp.concatenate([line[d * n1 : (d + 1) * n1], line[n2 + d * n1 : n2 + (d + 1) * n1]], axis=0)
        for d in range(SIDE)
    ]
    column_rows = added(dealt(line, first_axis, -1)).astype(jnp.bfloat16)
    sent = [
        jnp.concatenate(
            [column_rows[d * CAP : (d + 1) * CAP], column_rows[n1 + d * CAP : n1 + (d + 1) * CAP]],
            axis=0,
        )
        for d in range(SIDE)
    ]
    expert_rows = jnp.concatenate(dealt(sent, z_axis, -1), axis=0)
    picked = jnp.dot(match_table, expert_rows, preferred_element_type=jnp.float32).reshape(
        token_count, 2, -1
    )
    total = hidden_wide + route_gates[:, 0:1] * picked[:, 0] + route_gates[:, 1:2] * picked[:, 1]
    return total.astype(jnp.bfloat16)


def solution(mesh):
    return jax.shard_map(
        per_device,
        mesh=mesh,
        in_specs=(
            P("ctx", "exp"),
            P("ctx", "exp"),
            P("ctx", "exp"),
            P(),
            P(("ctx", "exp"), None),
            P("exp", "ctx"),
            P(),
            P(("ctx", "exp"), None),
            P(("ctx", "exp"), None),
            P("exp", None, "ctx"),
            P("exp", None, "ctx"),
            P("exp", "ctx", None),
        ),
        out_specs=P(("ctx", "exp"), None),
        check_vma=False,
    )
```

```python
import math

import jax
import jax.numpy as jnp
import numpy as np
from jax import lax
from jax.experimental import pallas as pl
from jax.experimental.pallas import tpu as pltpu
from jax.sharding import PartitionSpec as P

HEADS = 64
KV_HEADS = 8
HD = 128
CYCLE_STEPS = 4
CAP = 4
SIDE = 4
BOTH = ("ctx", "exp")
SHIFTS = (1, 3, 2)


def number(x, y, z, core):
    return (((x % SIDE) * SIDE + y % SIDE) * SIDE + z % SIDE) * 2 + core


def everyone():
    return [
        (x, y, z, core)
        for x in range(SIDE)
        for y in range(SIDE)
        for z in range(SIDE)
        for core in range(2)
    ]


def first_axis(d):
    return [
        (number(x, y, z, c), number(x + d * c, y + d * (1 - c), z, c)) for x, y, z, c in everyone()
    ]


def second_axis(d):
    return [
        (number(x, y, z, c), number(x + d * (1 - c), y + d * c, z, c)) for x, y, z, c in everyone()
    ]


def crossed(d):
    return [
        (number(x, y, z, c), number(x + d * (1 - c), y + d * c, z, 1 - c)) for x, y, z, c in everyone()
    ]


def uncrossed(d):
    return [(to, start) for start, to in crossed(d)]


def z_axis(d):
    return [(number(x, y, z, c), number(x, y, z + d, c)) for x, y, z, c in everyone()]


def sibling(shard):
    pairs = [(number(x, y, z, c), number(x, y, z, 1 - c)) for x, y, z, c in everyone()]
    return lax.ppermute(shard, BOTH, pairs)


def gathered(shard, along):
    got = {0: shard}
    for d in SHIFTS:
        got[d] = lax.ppermute(shard, BOTH, along(d))
    return [got[d] for d in range(SIDE)]


def dealt(blocks, along, sign):
    got = {0: blocks[0]}
    for d in SHIFTS:
        got[d] = lax.ppermute(blocks[d], BOTH, along(sign * d))
    return [got[d] for d in range(SIDE)]


def added(blocks):
    total = blocks[0].astype(jnp.float32)
    for block in blocks[1:]:
        total = total + block.astype(jnp.float32)
    return total


def expert_kernel(pieces, extra, *refs):
    x_refs = refs[:pieces]
    gate_ref, up_ref, down_ref = refs[pieces : pieces + 3]
    out_refs = refs[pieces + 3 + extra : 2 * pieces + 3 + extra]
    x_all = refs[2 * pieces + 3 + extra]
    piece = out_refs[0].shape[0]
    for i in range(pieces):
        x_all[i * piece : (i + 1) * piece, :] = x_refs[i][...]
    x = x_all[...]
    gate = jnp.dot(x, gate_ref[...], preferred_element_type=jnp.float32)
    up = jnp.dot(x, up_ref[...], preferred_element_type=jnp.float32)
    inner = (gate / (1.0 + jnp.exp(-gate)) * up).astype(jnp.bfloat16)
    part = jnp.dot(inner, down_ref[...], preferred_element_type=jnp.float32).astype(jnp.bfloat16)
    for i in range(pieces):
        out_refs[i][...] = part[i * piece : (i + 1) * piece]


def expert(xs, gate, up, down, after=()):
    width, hidden = gate.shape
    pieces = len(xs)
    piece = xs[0].shape[0]
    rows = pieces * piece
    vmem = pl.BlockSpec(memory_space=pltpu.VMEM)
    return pl.pallas_call(
        lambda *refs: expert_kernel(pieces, len(after), *refs),
        in_specs=[vmem] * (pieces + 3) + [pl.BlockSpec(memory_space=pl.ANY)] * len(after),
        out_specs=[vmem] * pieces,
        out_shape=[jax.ShapeDtypeStruct((piece, width), jnp.bfloat16)] * pieces,
        scratch_shapes=[pltpu.VMEM((rows, width), jnp.bfloat16)],
        compiler_params=pltpu.CompilerParams(vmem_limit_bytes=40 * 1024 * 1024),
        cost_estimate=pl.CostEstimate(
            flops=6 * rows * width * hidden,
            bytes_accessed=6 * width * hidden + 4 * rows * width,
            transcendentals=rows * hidden,
        ),
    )(*xs, gate, up, down, *after)


def per_device(
    queries,
    key_rows,
    values,
    span_order,
    residual,
    out_weight,
    norm_gain,
    routes,
    route_gates,
    gate_proj,
    up_proj,
    down_proj,
):
    n_ctx = lax.axis_size("ctx")
    n_exp = lax.axis_size("exp")
    here = lax.axis_index("ctx")
    column = lax.axis_index("exp")
    core = column % 2
    z_here = column // 2
    block_rows = queries.shape[0]
    group = HEADS // KV_HEADS
    kv_local = key_rows.shape[1] // HD
    width = kv_local * HD
    token_count, model = residual.shape
    offsets = jnp.arange(block_rows, dtype=jnp.int32)
    query_pos = span_order[here] * block_rows + offsets

    packed = jnp.concatenate([key_rows, values], axis=1)
    collected = [packed]
    positions = [query_pos]
    for step in range(1, CYCLE_STEPS):
        pairs = [(i, (i + step) % n_ctx) for i in range(n_ctx)]
        collected.append(lax.ppermute(packed, "ctx", pairs))
        positions.append(span_order[(here - step) % n_ctx] * block_rows + offsets)
    weight_other = sibling(out_weight)
    stacked = jnp.concatenate(collected, axis=0)
    key_all = stacked[:, :width].reshape(-1, kv_local, HD)
    value_all = stacked[:, width:].reshape(-1, kv_local, HD)
    key_pos = jnp.concatenate(positions)
    query_heads = queries.reshape(block_rows, kv_local, group, HD)
    scores = jnp.einsum(
        "qkgd,lkd->kgql", query_heads, key_all, preferred_element_type=jnp.float32
    ) * (1.0 / math.sqrt(HD))
    admitted = key_pos[None, :] <= query_pos[:, None]
    scores = jnp.where(admitted[None, None], scores, -1e30)
    row_max = jnp.max(scores, axis=-1, keepdims=True)
    exp_scores = jnp.exp(scores - row_max)
    attend_probs = (exp_scores / jnp.sum(exp_scores, axis=-1, keepdims=True)).astype(jnp.bfloat16)
    mixed = jnp.einsum(
        "kgql,lkd->qkgd", attend_probs, value_all, preferred_element_type=jnp.float32
    )
    attended = mixed.astype(jnp.bfloat16).reshape(SIDE, 2, token_count, kv_local * group * HD)

    half = SIDE * token_count
    rows_0 = attended[:, 0].reshape(half, -1)
    rows_1 = attended[:, 1].reshape(half, -1)
    kept = jnp.where(core == 0, rows_0, rows_1)
    given = jnp.where(core == 0, rows_1, rows_0)
    paired = jnp.concatenate([kept, sibling(given)], axis=1)
    weight = jnp.concatenate([out_weight, weight_other], axis=0)
    line = jnp.concatenate(gathered(paired, first_axis), axis=0)
    plane = jnp.concatenate(gathered(line, second_axis), axis=0)
    partial_value = jnp.dot(plane, weight, preferred_element_type=jnp.float32)
    columns = partial_value.shape[1]
    partial_value = partial_value.reshape(n_ctx, SIDE, token_count, columns)
    by_z = jnp.roll(jnp.moveaxis(partial_value, 1, 0), -z_here, axis=0)
    others = dealt([by_z[0]] + [by_z[d].astype(jnp.bfloat16) for d in range(1, SIDE)], z_axis, 1)
    slab = added(others).astype(jnp.bfloat16)
    x_here, y_here = here // SIDE, here % SIDE
    target = jnp.arange(n_ctx, dtype=jnp.int32)
    back_x = (x_here - target // SIDE) % SIDE
    back_y = (y_here - target % SIDE) % SIDE
    place = jnp.where(core == 0, back_x * SIDE + back_y, back_y * SIDE + back_x)
    slab = jnp.take(slab, place, axis=0)
    owned = lax.all_to_all(slab, "ctx", split_axis=0, concat_axis=0, tiled=True)
    projected = jnp.moveaxis(owned, 0, 1).reshape(token_count, model).astype(jnp.float32)
    hidden_wide = (
        (residual.astype(jnp.float32) + projected).astype(jnp.bfloat16).astype(jnp.float32)
    )
    inverse = lax.rsqrt(jnp.mean(hidden_wide * hidden_wide, axis=-1, keepdims=True) + 1e-06)
    normed = (hidden_wide * inverse * norm_gain.astype(jnp.float32)).astype(jnp.bfloat16)

    slots = n_exp * CAP
    flat_routes = routes.reshape(-1)
    pair_ids = jnp.arange(flat_routes.shape[0], dtype=jnp.int32)
    same_expert = flat_routes[:, None] == flat_routes[None, :]
    earlier = pair_ids[None, :] < pair_ids[:, None]
    slot_number = jnp.sum(jnp.where(same_expert & earlier, 1, 0), axis=1).astype(jnp.int32)
    ahead = (flat_routes // 2 - z_here) % SIDE
    target = (ahead * 2 + (flat_routes + core) % 2) * CAP + slot_number
    match_table = jnp.where(
        target[:, None] == jnp.arange(slots, dtype=jnp.int32)[None, :], 1.0, 0.0
    ).astype(jnp.bfloat16)
    assign = match_table.reshape(token_count, 2, slots).sum(axis=1)
    send_rows = jnp.einsum("ts,td->sd", assign, normed, preferred_element_type=jnp.float32).astype(
        jnp.bfloat16
    )
    per_z = 2 * CAP
    sent = dealt([send_rows[d * per_z : (d + 1) * per_z] for d in range(SIDE)], z_axis, 1)
    n1 = SIDE * CAP
    order = [k * per_z + part * CAP + i for part in range(2) for k in range(SIDE) for i in range(CAP)]
    reorder = jnp.asarray(np.eye(2 * n1)[order], jnp.bfloat16)
    column_rows = jnp.dot(
        reorder, jnp.concatenate(sent, axis=0), preferred_element_type=jnp.float32
    ).astype(jnp.bfloat16)
    line = gathered(column_rows, first_axis)
    own = jnp.concatenate([r[:n1] for r in line], axis=0)
    other = jnp.concatenate([r[n1:] for r in line], axis=0)
    mine, theirs = {0: own}, {0: sibling(other)}
    for d in (1, -1):
        mine[d] = lax.ppermute(own, BOTH, second_axis(d))
        theirs[d] = lax.ppermute(other, BOTH, crossed(d))
    mine[2] = lax.ppermute(mine[1], BOTH, second_axis(1))
    theirs[2] = lax.ppermute(theirs[-1], BOTH, first_axis(-1))
    weights = (gate_proj[0], up_proj[0], down_proj[0])
    sides = expert([mine[1], theirs[1], mine[-1], theirs[-1]], *weights)
    own, other = [], []
    for d, pair in ((1, sides[:2]), (-1, sides[2:])):
        own.append(lax.ppermute(pair[0], BOTH, second_axis(-d)))
        other.append(lax.ppermute(pair[1], BOTH, uncrossed(d)))
    far = expert([mine[2], theirs[2]], *weights, after=(sides[0],))
    own.append(lax.ppermute(far[0], BOTH, second_axis(-2)))
    other.append(lax.ppermute(far[1], BOTH, uncrossed(2)))
    near = expert([mine[0], theirs[0]], *weights, after=(far[0],))
    own.append(near[0])
    other.append(sibling(near[1]))
    line = jnp.concatenate([added(own), added(other)], axis=0).astype(jnp.bfloat16)
    n2 = SIDE * n1
    line = [
        jnp.concatenate([line[d * n1 : (d + 1) * n1], line[n2 + d * n1 : n2 + (d + 1) * n1]], axis=0)
        for d in range(SIDE)
    ]
    column_rows = added(dealt(line, first_axis, -1)).astype(jnp.bfloat16)
    sent = jnp.dot(reorder.T, column_rows, preferred_element_type=jnp.float32).astype(jnp.bfloat16)
    sent = [sent[d * per_z : (d + 1) * per_z] for d in range(SIDE)]
    expert_rows = jnp.concatenate(dealt(sent, z_axis, -1), axis=0)
    picked = jnp.dot(match_table, expert_rows, preferred_element_type=jnp.float32).reshape(
        token_count, 2, -1
    )
    total = hidden_wide + route_gates[:, 0:1] * picked[:, 0] + route_gates[:, 1:2] * picked[:, 1]
    return total.astype(jnp.bfloat16)


def solution(mesh):
    return jax.shard_map(
        per_device,
        mesh=mesh,
        in_specs=(
            P("ctx", "exp"),
            P("ctx", "exp"),
            P("ctx", "exp"),
            P(),
            P(("ctx", "exp"), None),
            P("exp", "ctx"),
            P(),
            P(("ctx", "exp"), None),
            P(("ctx", "exp"), None),
            P("exp", None, "ctx"),
            P("exp", None, "ctx"),
            P("exp", "ctx", None),
        ),
        out_specs=P(("ctx", "exp"), None),
        check_vma=False,
    )
```

```python
import math

import jax
import jax.numpy as jnp
from jax import lax
from jax.experimental import pallas as pl
from jax.experimental.pallas import tpu as pltpu
from jax.sharding import PartitionSpec as P

HEADS = 64
KV_HEADS = 8
HD = 128
CYCLE_STEPS = 4
CAP = 4
SIDE = 4
BOTH = ("ctx", "exp")
SHIFTS = (1, 3, 2)


def number(x, y, z, core):
    return (((x % SIDE) * SIDE + y % SIDE) * SIDE + z % SIDE) * 2 + core


def everyone():
    return [
        (x, y, z, core)
        for x in range(SIDE)
        for y in range(SIDE)
        for z in range(SIDE)
        for core in range(2)
    ]


def first_axis(d):
    return [
        (number(x, y, z, c), number(x + d * c, y + d * (1 - c), z, c)) for x, y, z, c in everyone()
    ]


def second_axis(d):
    return [
        (number(x, y, z, c), number(x + d * (1 - c), y + d * c, z, c)) for x, y, z, c in everyone()
    ]


def crossed(d):
    return [
        (number(x, y, z, c), number(x + d * (1 - c), y + d * c, z, 1 - c)) for x, y, z, c in everyone()
    ]


def uncrossed(d):
    return [(to, start) for start, to in crossed(d)]


def z_axis(d):
    return [(number(x, y, z, c), number(x, y, z + d, c)) for x, y, z, c in everyone()]


def z_exchange(bit):
    return [(number(x, y, z, c), number(x, y, z ^ bit, c)) for x, y, z, c in everyone()]


def sibling(shard):
    pairs = [(number(x, y, z, c), number(x, y, z, 1 - c)) for x, y, z, c in everyone()]
    return lax.ppermute(shard, BOTH, pairs)


def gathered(shard, along):
    got = {0: shard}
    for d in SHIFTS:
        got[d] = lax.ppermute(shard, BOTH, along(d))
    return [got[d] for d in range(SIDE)]


def dealt(blocks, along, sign):
    got = {0: blocks[0]}
    for d in SHIFTS:
        got[d] = lax.ppermute(blocks[d], BOTH, along(sign * d))
    return [got[d] for d in range(SIDE)]


def added(blocks):
    total = blocks[0].astype(jnp.float32)
    for block in blocks[1:]:
        total = total + block.astype(jnp.float32)
    return total


def whole(*names):
    spaces = {"v": pltpu.VMEM, "s": pltpu.SMEM}
    return [pl.BlockSpec(memory_space=spaces[n]) for n in names]


def project_kernel(where, place, p0, p1, p2, p3, w0, w1, res, codes_ref, spread, wide, named_by):
    depth = w0.shape[0]
    for k2, piece in enumerate((p0, p1, p2, p3)):
        part = jnp.dot(piece[:, :depth], w0[...], preferred_element_type=jnp.float32)
        part += jnp.dot(piece[:, depth : 2 * depth], w1[...], preferred_element_type=jnp.float32)
        for k1 in range(SIDE):
            at = place[k2 * SIDE + k1]
            residual = res[at].astype(jnp.float32)
            for zt in range(SIDE):
                lo = (k1 * SIDE + zt) * 8
                seg = part[lo : lo + 8]
                named_by[lo : lo + 8] = codes_ref[zt ^ where[2], at].astype(jnp.float32)
                wide[lo : lo + 8] = seg + jnp.where(zt == where[2], residual, 0.0)
        rows = wide[...].astype(jnp.bfloat16)
        codes = named_by[...]
        shape = (rows.shape[0], 16 * 2 * SIDE * CAP)
        slot = lax.broadcasted_iota(jnp.int32, shape, 1)
        group = lax.broadcasted_iota(jnp.int32, shape, 0) // 8
        code = ((slot // 64) * CAP + slot % CAP).astype(jnp.float32)
        named = jnp.logical_or(codes[:, 0:1] == code, codes[:, 1:2] == code)
        hit = jnp.logical_and(named, (slot % 64) // CAP == group)
        table = jnp.where(hit, 1.0, 0.0).astype(jnp.bfloat16)
        chosen = lax.dot_general(
            table, rows, (((0,), (0,)), ((), ())), preferred_element_type=jnp.float32
        ).astype(spread.dtype)
        i2 = (where[0] - k2 + SIDE) % SIDE
        for zt in range(SIDE):
            ahead = (zt - where[2] + SIDE) % SIDE
            for p in range(2):
                for k1 in range(SIDE):
                    lo = (zt * 2 + p) * 64 + k1 * 16
                    spread[ahead, p, i2, (where[1] - k1 + SIDE) % SIDE] = chosen[lo : lo + 16]


def project(where, place, pieces, w0, w1, res, codes):
    columns = w0.shape[1]
    return pl.pallas_call(
        project_kernel,
        in_specs=whole(*"ssvvvvvvvv"),
        out_specs=whole("v")[0],
        out_shape=jax.ShapeDtypeStruct((SIDE, 2, SIDE, SIDE, 4 * CAP, columns), jnp.bfloat16),
        scratch_shapes=[
            pltpu.VMEM((pieces[0].shape[0], columns), jnp.float32),
            pltpu.VMEM((pieces[0].shape[0], HD), jnp.float32),
        ],
        compiler_params=pltpu.CompilerParams(vmem_limit_bytes=16 * 1024 * 1024),
        cost_estimate=pl.CostEstimate(
            flops=2 * 512 * 2048 * 256 + 2 * 2048 * 128 * 256,
            bytes_accessed=6 * 1024 * 1024,
            transcendentals=0,
        ),
    )(where, place, *pieces, w0, w1, res, codes)


def hidden_step(blocks, at, row, gate_ref, up_ref, gain_ref, gate_in, up_in, sq_in, outs):
    gate_out, up_out, sq_out = outs
    rows = pl.ds(row, 256)
    gate = up = sq = None
    for block, c in zip(blocks, at):
        wide = block.astype(jnp.float32)
        square = wide * wide
        square = square[:, :128] + square[:, 128:]
        x = (wide * gain_ref[c]).astype(jnp.bfloat16)
        k = pl.ds(pl.multiple_of(c * 256, 256), 256)
        g = jnp.dot(x, gate_ref[k, :], preferred_element_type=jnp.float32)
        u = jnp.dot(x, up_ref[k, :], preferred_element_type=jnp.float32)
        gate = g if gate is None else gate + g
        up = u if up is None else up + u
        sq = square if sq is None else sq + square
    if gate_in is not None:
        gate, up, sq = gate + gate_in[rows], up + up_in[rows], sq + sq_in[rows]
    gate_out[rows], up_out[rows], sq_out[rows] = gate, up, sq


def first_kernel(count, has_sums, *refs):
    at_ref = refs[0]
    shards = refs[1 : 1 + 2 * count]
    gain_ref, gate_ref, up_ref = refs[1 + 2 * count : 4 + 2 * count]
    sums = refs[4 + 2 * count : 7 + 2 * count] if has_sums else (None, None, None)
    outs = refs[-3:]
    for half in range(2):
        blocks = [shards[half * count + i][k] for i in range(count) for k in range(SIDE)]
        at = [at_ref[(half * count + i) * SIDE + k] for i in range(count) for k in range(SIDE)]
        hidden_step(blocks, at, half * 256, gate_ref, up_ref, gain_ref, *sums, outs)


def first_products(at, mine, theirs, gain, gate, up, sums=()):
    count = len(mine)
    hidden = gate.shape[1]
    wide = jax.ShapeDtypeStruct((512, hidden), jnp.float32)
    return pl.pallas_call(
        lambda *refs: first_kernel(count, bool(sums), *refs),
        in_specs=whole("s", *("v" * (2 * count + 3 + len(sums)))),
        out_specs=whole(*"vvv"),
        out_shape=[wide, wide, jax.ShapeDtypeStruct((512, 128), jnp.float32)],
        input_output_aliases={4 + 2 * count + i: i for i in range(len(sums))},
        compiler_params=pltpu.CompilerParams(vmem_limit_bytes=12 * 1024 * 1024),
        cost_estimate=pl.CostEstimate(
            flops=4 * 512 * 1024 * count * hidden,
            bytes_accessed=4096 * count * hidden,
            transcendentals=0,
        ),
    )(at, *mine, *theirs, gain, gate, up, *sums)


def last_kernel(width, at_ref, mine, theirs, gain, gate_w, up_w, gate_in, up_in, sq_in, down, where, *refs):
    out_mine, out_theirs, rest, gate, up, sq, inner = refs
    for half, shard in enumerate((mine, theirs)):
        blocks = [shard[k] for k in range(SIDE)]
        at = [at_ref[half * SIDE + k] for k in range(SIDE)]
        hidden_step(blocks, at, half * 256, gate_w, up_w, gain, gate_in, up_in, sq_in, (gate, up, sq))
    for half in range(2):
        rows = pl.ds(half * 256, 256)
        mean = jnp.sum(sq[rows], axis=1, keepdims=True) * (1.0 / width)
        scale = lax.rsqrt(mean + 1e-06)
        g = gate[rows] * scale
        u = up[rows] * scale
        act = (g / (1.0 + jnp.exp(-g)) * u).astype(jnp.bfloat16)
        for i in range(16):
            inner[half * 16 + i] = act[i * 16 : (i + 1) * 16]
    for half in range(2):
        for d in range(SIDE):
            i2 = (where[half] - d + SIDE) % SIDE
            for j in range(SIDE):
                i1 = (where[1 - half] - j + SIDE) % SIDE
                rest[((d * 2 + half) * SIDE + j) * 16 : ((d * 2 + half) * SIDE + j + 1) * 16, :] = inner[
                    half * 16 + i2 * SIDE + i1
                ]
    part = jnp.dot(rest[256:384, :], down[...], preferred_element_type=jnp.float32)
    part = part.astype(jnp.bfloat16)
    out_mine[...] = part[:64]
    out_theirs[...] = part[64:]


def last_products(at, mine, theirs, gain, gate, up, sums, down, where):
    hidden, width = down.shape
    return pl.pallas_call(
        lambda *refs: last_kernel(width, *refs),
        in_specs=whole(*"svvvvvvvvvs"),
        out_specs=whole(*"vvv"),
        out_shape=[jax.ShapeDtypeStruct((64, width), jnp.bfloat16)] * 2
        + [jax.ShapeDtypeStruct((512, hidden), jnp.bfloat16)],
        scratch_shapes=[
            pltpu.VMEM((512, hidden), jnp.float32),
            pltpu.VMEM((512, hidden), jnp.float32),
            pltpu.VMEM((512, 128), jnp.float32),
            pltpu.VMEM((32, 16, hidden), jnp.bfloat16),
        ],
        compiler_params=pltpu.CompilerParams(vmem_limit_bytes=16 * 1024 * 1024),
        cost_estimate=pl.CostEstimate(
            flops=4 * 512 * 1024 * hidden + 2 * 128 * hidden * width,
            bytes_accessed=4096 * hidden + 2 * hidden * width,
            transcendentals=512 * hidden,
        ),
    )(at, mine, theirs, gain, gate, up, *sums, down, where)


def down_kernel(picks, inner, down, after, *outs):
    for i, d in enumerate(picks):
        part = jnp.dot(
            inner[d * 128 : (d + 1) * 128, :], down[...], preferred_element_type=jnp.float32
        ).astype(jnp.bfloat16)
        outs[2 * i][...] = part[:64]
        outs[2 * i + 1][...] = part[64:]


def down_products(picks, inner, down, after):
    hidden, width = down.shape
    return pl.pallas_call(
        lambda *refs: down_kernel(picks, *refs),
        in_specs=whole(*"vv") + [pl.BlockSpec(memory_space=pl.ANY)],
        out_specs=whole(*("vv" * len(picks))),
        out_shape=[jax.ShapeDtypeStruct((64, width), jnp.bfloat16)] * (2 * len(picks)),
        compiler_params=pltpu.CompilerParams(vmem_limit_bytes=10 * 1024 * 1024),
        cost_estimate=pl.CostEstimate(
            flops=2 * 128 * len(picks) * hidden * width,
            bytes_accessed=2 * hidden * width,
            transcendentals=0,
        ),
    )(inner, down, after)


def pack_kernel(terms, *refs):
    outs = refs[2 * terms :]
    for half in range(2):
        total = refs[half * terms][...].astype(jnp.float32)
        for i in range(1, terms):
            total = total + refs[half * terms + i][...].astype(jnp.float32)
        total = total.astype(jnp.bfloat16)
        for d in range(SIDE):
            outs[d][half * 16 : half * 16 + 16, :] = total[d * 16 : (d + 1) * 16]


def packed_sums(own, other):
    terms, width = len(own), own[0].shape[1]
    return pl.pallas_call(
        lambda *refs: pack_kernel(terms, *refs),
        in_specs=whole(*("v" * 2 * terms)),
        out_specs=whole(*("v" * SIDE)),
        out_shape=[jax.ShapeDtypeStruct((32, width), jnp.bfloat16)] * SIDE,
        compiler_params=pltpu.CompilerParams(vmem_limit_bytes=12582912),
    )(*own, *other)


def pick_kernel(at_ref, where, *refs):
    shards, outs = refs[: 2 * SIDE], refs[-2:]
    for half in range(2):
        for i in range(SIDE):
            for k in range(SIDE):
                columns = pl.ds(pl.multiple_of(at_ref[i * 2 * SIDE + half * SIDE + k] * 256, 256), 256)
                shard = shards[half * SIDE + i]
                outs[half][:, columns] = shard[k, where[half] * SIDE + where[1 - half]]


def pick_hidden(at, where, shards, after):
    shards = [r.reshape(SIDE, 16, 16, r.shape[-1]) for r in shards]
    return pl.pallas_call(
        pick_kernel,
        in_specs=whole("s", "s", *("v" * len(shards))) + [pl.BlockSpec(memory_space=pl.ANY)],
        out_specs=whole(*"vv"),
        out_shape=[jax.ShapeDtypeStruct((16, 16 * shards[0].shape[-1]), jnp.bfloat16)] * 2,
        compiler_params=pltpu.CompilerParams(vmem_limit_bytes=8 * 1024 * 1024),
    )(at, where, *shards, after)


def per_device(
    queries,
    key_rows,
    values,
    span_order,
    residual,
    out_weight,
    norm_gain,
    routes,
    route_gates,
    gate_proj,
    up_proj,
    down_proj,
):
    n_ctx = lax.axis_size("ctx")
    n_exp = lax.axis_size("exp")
    here = lax.axis_index("ctx")
    column = lax.axis_index("exp")
    core = column % 2
    z_here = column // 2
    block_rows = queries.shape[0]
    group = HEADS // KV_HEADS
    kv_local = key_rows.shape[1] // HD
    width = kv_local * HD
    token_count, model = residual.shape
    offsets = jnp.arange(block_rows, dtype=jnp.int32)
    back_places = (here - jnp.arange(CYCLE_STEPS, dtype=jnp.int32)) % n_ctx
    picked_place = back_places[:, None] == jnp.arange(n_ctx, dtype=jnp.int32)[None, :]
    starts = jnp.sum(jnp.where(picked_place, span_order[None, :], 0), axis=1) * block_rows
    key_pos = (starts[:, None] + offsets[None, :]).reshape(-1)
    query_pos = jnp.sum(jnp.where(picked_place[0], span_order, 0)) * block_rows + offsets

    packed = jnp.pad(key_rows, ((0, 0), (0, width))) + jnp.pad(values, ((0, 0), (width, 0)))

    def onward(shard, step):
        return lax.ppermute(shard, "ctx", [(i, (i + step) % n_ctx) for i in range(n_ctx)])

    collected = [packed] + [onward(packed, step) for step in range(1, CYCLE_STEPS)]
    flat_routes = routes.reshape(-1)
    pair_ids = jnp.arange(flat_routes.shape[0], dtype=jnp.int32)
    same_expert = flat_routes[:, None] == flat_routes[None, :]
    earlier = pair_ids[None, :] < pair_ids[:, None]
    slot_number = jnp.sum(jnp.where(same_expert & earlier, 1, 0), axis=1).astype(jnp.int32)
    other_core = (flat_routes + core) % 2
    codes = ((flat_routes // 2 * 2 + other_core) * CAP + slot_number).astype(jnp.bfloat16)
    codes = jnp.pad(codes.reshape(token_count, 2), ((0, 0), (0, HD - 2)))
    z_places = jnp.arange(SIDE, dtype=jnp.int32)
    columns = out_weight.shape[1]
    by_column = jnp.moveaxis(residual.reshape(token_count, n_ctx, columns), 1, 0)
    by_column = jnp.concatenate(
        [by_column, jnp.broadcast_to(codes[None], (n_ctx, token_count, HD))], axis=2
    )
    by_column = lax.all_to_all(by_column, "ctx", split_axis=0, concat_axis=0, tiled=True)
    residual_slab = by_column[:, :, :columns]
    codes = by_column[None, :, :, columns:]
    codes = jnp.concatenate([codes, lax.ppermute(codes, BOTH, z_exchange(1))], axis=0)
    codes = jnp.concatenate([codes, lax.ppermute(codes, BOTH, z_exchange(2))], axis=0)
    weight_other = sibling(out_weight)
    stacked = jnp.concatenate(collected, axis=0)
    key_all = stacked[:, :width].reshape(-1, kv_local, HD)
    value_all = stacked[:, width:].reshape(-1, kv_local, HD)
    query_heads = queries.reshape(block_rows, kv_local, group, HD)
    scores = jnp.einsum(
        "qkgd,lkd->kgql", query_heads, key_all, preferred_element_type=jnp.float32
    ) * (1.0 / math.sqrt(HD))
    admitted = key_pos[None, :] <= query_pos[:, None]
    scores = jnp.where(admitted[None, None], scores, -1e30)
    row_max = jnp.max(scores, axis=-1, keepdims=True)
    exp_scores = jnp.exp(scores - row_max)
    attend_probs = (exp_scores / jnp.sum(exp_scores, axis=-1, keepdims=True)).astype(jnp.bfloat16)
    mixed = jnp.einsum(
        "kgql,lkd->qkgd", attend_probs, value_all, preferred_element_type=jnp.float32
    )
    attended = mixed.astype(jnp.bfloat16).reshape(SIDE, 2, token_count, kv_local * group * HD)

    half = SIDE * token_count
    rows_0 = attended[:, 0].reshape(half, -1)
    rows_1 = attended[:, 1].reshape(half, -1)
    kept = jnp.where(core == 0, rows_0, rows_1)
    given = jnp.where(core == 0, rows_1, rows_0)
    paired = jnp.concatenate([kept, sibling(given)], axis=1)
    line = jnp.concatenate(gathered(paired, first_axis), axis=0)
    plane = gathered(line, second_axis)

    x_here, y_here = here // SIDE, here % SIDE
    second = jnp.where(core == 0, x_here, y_here)
    first = jnp.where(core == 0, y_here, x_here)
    where = jnp.stack([second, first, z_here]).astype(jnp.int32)
    k2, k1 = z_places[:, None], z_places[None, :]
    by_x = ((x_here - k2) % SIDE * SIDE + (y_here - k1) % SIDE).astype(jnp.int32)
    by_y = ((x_here - k1) % SIDE * SIDE + (y_here - k2) % SIDE).astype(jnp.int32)
    place = jnp.where(core == 0, by_x, by_y)
    place_other = jnp.where(core == 0, by_y, by_x)
    spread = project(
        where, place.reshape(-1), plane, out_weight, weight_other, residual_slab, codes
    )

    rows = added(dealt([spread[d] for d in range(SIDE)], z_axis, 1)).astype(jnp.bfloat16)
    rows = rows.reshape(2, SIDE * SIDE * SIDE * CAP, columns)
    line = gathered(rows, first_axis)
    own = jnp.stack([r[0] for r in line])
    other = jnp.stack([r[1] for r in line])
    mine, theirs = {0: own}, {0: sibling(other)}
    for d in (1, -1):
        mine[d] = lax.ppermute(own, BOTH, second_axis(d))
        theirs[d] = lax.ppermute(other, BOTH, crossed(d))
    gain = norm_gain.astype(jnp.float32).reshape(n_ctx, 1, columns)
    gate_w, up_w, down_w = gate_proj[0], up_proj[0], down_proj[0]

    def at(*shifts):
        return jnp.concatenate([place[d] for d in shifts] + [place_other[d] for d in shifts])

    near = first_products(at(0), [mine[0]], [theirs[0]], gain, gate_w, up_w)
    on_mine, on_theirs, *near = lax.optimization_barrier((mine[1], theirs[-1], *near))
    mine[2] = lax.ppermute(on_mine, BOTH, second_axis(1))
    theirs[2] = lax.ppermute(on_theirs, BOTH, first_axis(-1))
    sides = first_products(
        at(1, 3), [mine[1], mine[-1]], [theirs[1], theirs[-1]], gain, gate_w, up_w, tuple(near)
    )
    far_mine, far_theirs, inner = last_products(
        at(2), mine[2], theirs[2], gain, gate_w, up_w, tuple(sides), down_w, where
    )
    side_out = down_products((1, 3), inner, down_w, far_mine)
    far_mine = lax.ppermute(far_mine, BOTH, second_axis(-1))
    far_theirs = lax.ppermute(far_theirs, BOTH, first_axis(1))
    near_out = down_products((0,), inner, down_w, far_theirs)
    back_mine, back_theirs, front_mine, front_theirs = side_out
    own = [near_out[0], lax.ppermute(front_mine, BOTH, second_axis(1))]
    other = [sibling(near_out[1]), lax.ppermute(back_theirs, BOTH, uncrossed(1))]
    back_mine = added([back_mine, far_mine]).astype(jnp.bfloat16)
    front_theirs = added([front_theirs, far_theirs]).astype(jnp.bfloat16)
    own.append(lax.ppermute(back_mine, BOTH, second_axis(-1)))
    other.append(lax.ppermute(front_theirs, BOTH, uncrossed(-1)))
    line = packed_sums(own, other)
    n1 = SIDE * CAP

    names = (0, 1, -1, 2)
    hidden_mine, hidden_theirs = pick_hidden(
        jnp.concatenate([at(0), at(1), at(3), at(2)]),
        where,
        [mine[d] for d in names] + [theirs[d] for d in names],
        side_out[0],
    )
    hidden_rows = jnp.concatenate([hidden_mine, sibling(hidden_theirs)], axis=0)
    slots = n_exp * CAP
    ahead = (flat_routes // 2 - z_here) % SIDE
    target = (ahead * 2 + other_core) * CAP + slot_number
    match_table = jnp.where(
        target[:, None] == jnp.arange(slots, dtype=jnp.int32)[None, :], 1.0, 0.0
    ).astype(jnp.bfloat16)
    per_z = 2 * CAP
    column_rows = added(dealt(line, first_axis, -1)).astype(jnp.bfloat16)
    row = jnp.arange(slots, dtype=jnp.int32)
    source = (row // CAP % 2) * n1 + (z_here - row // per_z) % SIDE * CAP + row % CAP
    reorder = jnp.where(source[:, None] == row[None, :], 1.0, 0.0).astype(jnp.bfloat16)
    column_rows = jnp.concatenate([column_rows, hidden_rows], axis=1)
    sent = jnp.dot(reorder, column_rows, preferred_element_type=jnp.float32).astype(jnp.bfloat16)
    sent = [sent[d * per_z : (d + 1) * per_z] for d in range(SIDE)]
    expert_rows = jnp.concatenate(dealt(sent, z_axis, -1), axis=0)
    picked = jnp.dot(match_table, expert_rows, preferred_element_type=jnp.float32).reshape(
        token_count, 2, -1
    )
    total = (
        picked[:, 0, model:]
        + route_gates[:, 0:1] * picked[:, 0, :model]
        + route_gates[:, 1:2] * picked[:, 1, :model]
    )
    return total.astype(jnp.bfloat16)


def solution(mesh):
    return jax.shard_map(
        per_device,
        mesh=mesh,
        in_specs=(
            P("ctx", "exp"),
            P("ctx", "exp"),
            P("ctx", "exp"),
            P(),
            P(("ctx", "exp"), None),
            P("exp", "ctx"),
            P(),
            P(("ctx", "exp"), None),
            P(("ctx", "exp"), None),
            P("exp", None, "ctx"),
            P("exp", None, "ctx"),
            P("exp", "ctx", None),
        ),
        out_specs=P(("ctx", "exp"), None),
        check_vma=False,
    )
```

```python
import math

import jax
import jax.numpy as jnp
from jax import lax
from jax.experimental import pallas as pl
from jax.experimental.pallas import tpu as pltpu
from jax.sharding import PartitionSpec as P

HEADS = 64
KV_HEADS = 8
HD = 128
CYCLE_STEPS = 4
CAP = 4
SIDE = 4
BOTH = ("ctx", "exp")
SHIFTS = (1, 3, 2)


def number(x, y, z, core):
    return (((x % SIDE) * SIDE + y % SIDE) * SIDE + z % SIDE) * 2 + core


def everyone():
    return [
        (x, y, z, core)
        for x in range(SIDE)
        for y in range(SIDE)
        for z in range(SIDE)
        for core in range(2)
    ]


def first_axis(d):
    return [
        (number(x, y, z, c), number(x + d * c, y + d * (1 - c), z, c)) for x, y, z, c in everyone()
    ]


def second_axis(d):
    return [
        (number(x, y, z, c), number(x + d * (1 - c), y + d * c, z, c)) for x, y, z, c in everyone()
    ]


def crossed(d):
    return [
        (number(x, y, z, c), number(x + d * (1 - c), y + d * c, z, 1 - c)) for x, y, z, c in everyone()
    ]


def uncrossed(d):
    return [(to, start) for start, to in crossed(d)]


def z_axis(d):
    return [(number(x, y, z, c), number(x, y, z + d, c)) for x, y, z, c in everyone()]


def z_exchange(bit):
    return [(number(x, y, z, c), number(x, y, z ^ bit, c)) for x, y, z, c in everyone()]


def sibling(shard):
    pairs = [(number(x, y, z, c), number(x, y, z, 1 - c)) for x, y, z, c in everyone()]
    return lax.ppermute(shard, BOTH, pairs)


def gathered(shard, along):
    got = {0: shard}
    for d in SHIFTS:
        got[d] = lax.ppermute(shard, BOTH, along(d))
    return [got[d] for d in range(SIDE)]


def dealt(blocks, along, sign):
    got = {0: blocks[0]}
    for d in SHIFTS:
        got[d] = lax.ppermute(blocks[d], BOTH, along(sign * d))
    return [got[d] for d in range(SIDE)]


def added(blocks):
    total = blocks[0].astype(jnp.float32)
    for block in blocks[1:]:
        total = total + block.astype(jnp.float32)
    return total


def whole(*names):
    spaces = {"v": pltpu.VMEM, "s": pltpu.SMEM}
    return [pl.BlockSpec(memory_space=spaces[n]) for n in names]


def project_kernel(where, place, p0, p1, p2, p3, w0, w1, res, codes_ref, spread, wide, named_by):
    depth = w0.shape[0]
    for k2, piece in enumerate((p0, p1, p2, p3)):
        part = jnp.dot(piece[:, :depth], w0[...], preferred_element_type=jnp.float32)
        part += jnp.dot(piece[:, depth : 2 * depth], w1[...], preferred_element_type=jnp.float32)
        for k1 in range(SIDE):
            at = place[k2 * SIDE + k1]
            residual = res[at].astype(jnp.float32)
            for zt in range(SIDE):
                lo = (k1 * SIDE + zt) * 8
                seg = part[lo : lo + 8]
                named_by[lo : lo + 8] = codes_ref[zt ^ where[2], at].astype(jnp.float32)
                wide[lo : lo + 8] = seg + jnp.where(zt == where[2], residual, 0.0)
        rows = wide[...].astype(jnp.bfloat16)
        codes = named_by[...]
        shape = (rows.shape[0], 16 * 2 * SIDE * CAP)
        slot = lax.broadcasted_iota(jnp.int32, shape, 1)
        group = lax.broadcasted_iota(jnp.int32, shape, 0) // 8
        code = ((slot // 64) * CAP + slot % CAP).astype(jnp.float32)
        named = jnp.logical_or(codes[:, 0:1] == code, codes[:, 1:2] == code)
        hit = jnp.logical_and(named, (slot % 64) // CAP == group)
        table = jnp.where(hit, 1.0, 0.0).astype(jnp.bfloat16)
        chosen = lax.dot_general(
            table, rows, (((0,), (0,)), ((), ())), preferred_element_type=jnp.float32
        ).astype(spread.dtype)
        i2 = (where[0] - k2 + SIDE) % SIDE
        for zt in range(SIDE):
            ahead = (zt - where[2] + SIDE) % SIDE
            for p in range(2):
                for k1 in range(SIDE):
                    lo = (zt * 2 + p) * 64 + k1 * 16
                    spread[ahead, p, i2, (where[1] - k1 + SIDE) % SIDE] = chosen[lo : lo + 16]


def project(where, place, pieces, w0, w1, res, codes):
    columns = w0.shape[1]
    return pl.pallas_call(
        project_kernel,
        in_specs=whole(*"ssvvvvvvvv"),
        out_specs=whole("v")[0],
        out_shape=jax.ShapeDtypeStruct((SIDE, 2, SIDE, SIDE, 4 * CAP, columns), jnp.bfloat16),
        scratch_shapes=[
            pltpu.VMEM((pieces[0].shape[0], columns), jnp.float32),
            pltpu.VMEM((pieces[0].shape[0], HD), jnp.float32),
        ],
        compiler_params=pltpu.CompilerParams(vmem_limit_bytes=16 * 1024 * 1024),
        cost_estimate=pl.CostEstimate(
            flops=2 * 512 * 2048 * 256 + 2 * 2048 * 128 * 256,
            bytes_accessed=6 * 1024 * 1024,
            transcendentals=0,
        ),
    )(where, place, *pieces, w0, w1, res, codes)


def hidden_step(blocks, at, row, gate_ref, up_ref, gain_ref, gate_in, up_in, sq_in, outs):
    gate_out, up_out, sq_out = outs
    rows = pl.ds(row, 256)
    gate = up = sq = None
    for block, c in zip(blocks, at):
        wide = block.astype(jnp.float32)
        square = wide * wide
        square = square[:, :128] + square[:, 128:]
        x = (wide * gain_ref[c]).astype(jnp.bfloat16)
        k = pl.ds(pl.multiple_of(c * 256, 256), 256)
        g = jnp.dot(x, gate_ref[k, :], preferred_element_type=jnp.float32)
        u = jnp.dot(x, up_ref[k, :], preferred_element_type=jnp.float32)
        gate = g if gate is None else gate + g
        up = u if up is None else up + u
        sq = square if sq is None else sq + square
    if gate_in is not None:
        gate, up, sq = gate + gate_in[rows], up + up_in[rows], sq + sq_in[rows]
    gate_out[rows], up_out[rows], sq_out[rows] = gate, up, sq


def first_kernel(count, has_sums, *refs):
    at_ref = refs[0]
    shards = refs[1 : 1 + 2 * count]
    gain_ref, gate_ref, up_ref = refs[1 + 2 * count : 4 + 2 * count]
    sums = refs[4 + 2 * count : 7 + 2 * count] if has_sums else (None, None, None)
    outs = refs[-3:]
    for half in range(2):
        blocks = [shards[half * count + i][k] for i in range(count) for k in range(SIDE)]
        at = [at_ref[(half * count + i) * SIDE + k] for i in range(count) for k in range(SIDE)]
        hidden_step(blocks, at, half * 256, gate_ref, up_ref, gain_ref, *sums, outs)


def first_products(at, mine, theirs, gain, gate, up, sums=()):
    count = len(mine)
    hidden = gate.shape[1]
    wide = jax.ShapeDtypeStruct((512, hidden), jnp.float32)
    return pl.pallas_call(
        lambda *refs: first_kernel(count, bool(sums), *refs),
        in_specs=whole("s", *("v" * (2 * count + 3 + len(sums)))),
        out_specs=whole(*"vvv"),
        out_shape=[wide, wide, jax.ShapeDtypeStruct((512, 128), jnp.float32)],
        input_output_aliases={4 + 2 * count + i: i for i in range(len(sums))},
        compiler_params=pltpu.CompilerParams(vmem_limit_bytes=12 * 1024 * 1024),
        cost_estimate=pl.CostEstimate(
            flops=4 * 512 * 1024 * count * hidden,
            bytes_accessed=4096 * count * hidden,
            transcendentals=0,
        ),
    )(at, *mine, *theirs, gain, gate, up, *sums)


def last_kernel(width, at_ref, mine, theirs, gain, gate_w, up_w, gate_in, up_in, sq_in, down, where, *refs):
    out_mine, out_theirs, rest, gate, up, sq, inner = refs
    for half, shard in enumerate((mine, theirs)):
        blocks = [shard[k] for k in range(SIDE)]
        at = [at_ref[half * SIDE + k] for k in range(SIDE)]
        hidden_step(blocks, at, half * 256, gate_w, up_w, gain, gate_in, up_in, sq_in, (gate, up, sq))
    for half in range(2):
        rows = pl.ds(half * 256, 256)
        mean = jnp.sum(sq[rows], axis=1, keepdims=True) * (1.0 / width)
        scale = lax.rsqrt(mean + 1e-06)
        g = gate[rows] * scale
        u = up[rows] * scale
        act = (g / (1.0 + jnp.exp(-g)) * u).astype(jnp.bfloat16)
        for i in range(16):
            inner[half * 16 + i] = act[i * 16 : (i + 1) * 16]
    for half in range(2):
        for d in range(SIDE):
            i2 = (where[half] - d + SIDE) % SIDE
            for j in range(SIDE):
                i1 = (where[1 - half] - j + SIDE) % SIDE
                rest[((d * 2 + half) * SIDE + j) * 16 : ((d * 2 + half) * SIDE + j + 1) * 16, :] = inner[
                    half * 16 + i2 * SIDE + i1
                ]
    part = jnp.dot(rest[256:384, :], down[...], preferred_element_type=jnp.float32)
    part = part.astype(jnp.bfloat16)
    out_mine[...] = part[:64]
    out_theirs[...] = part[64:]


def last_products(at, mine, theirs, gain, gate, up, sums, down, where):
    hidden, width = down.shape
    return pl.pallas_call(
        lambda *refs: last_kernel(width, *refs),
        in_specs=whole(*"svvvvvvvvvs"),
        out_specs=whole(*"vvv"),
        out_shape=[jax.ShapeDtypeStruct((64, width), jnp.bfloat16)] * 2
        + [jax.ShapeDtypeStruct((512, hidden), jnp.bfloat16)],
        scratch_shapes=[
            pltpu.VMEM((512, hidden), jnp.float32),
            pltpu.VMEM((512, hidden), jnp.float32),
            pltpu.VMEM((512, 128), jnp.float32),
            pltpu.VMEM((32, 16, hidden), jnp.bfloat16),
        ],
        compiler_params=pltpu.CompilerParams(vmem_limit_bytes=16 * 1024 * 1024),
        cost_estimate=pl.CostEstimate(
            flops=4 * 512 * 1024 * hidden + 2 * 128 * hidden * width,
            bytes_accessed=4096 * hidden + 2 * hidden * width,
            transcendentals=512 * hidden,
        ),
    )(at, mine, theirs, gain, gate, up, *sums, down, where)


def down_kernel(picks, inner, down, after, *outs):
    for i, d in enumerate(picks):
        part = jnp.dot(
            inner[d * 128 : (d + 1) * 128, :], down[...], preferred_element_type=jnp.float32
        ).astype(jnp.bfloat16)
        outs[2 * i][...] = part[:64]
        outs[2 * i + 1][...] = part[64:]


def down_products(picks, inner, down, after):
    hidden, width = down.shape
    return pl.pallas_call(
        lambda *refs: down_kernel(picks, *refs),
        in_specs=whole(*"vv") + [pl.BlockSpec(memory_space=pl.ANY)],
        out_specs=whole(*("vv" * len(picks))),
        out_shape=[jax.ShapeDtypeStruct((64, width), jnp.bfloat16)] * (2 * len(picks)),
        compiler_params=pltpu.CompilerParams(vmem_limit_bytes=10 * 1024 * 1024),
        cost_estimate=pl.CostEstimate(
            flops=2 * 128 * len(picks) * hidden * width,
            bytes_accessed=2 * hidden * width,
            transcendentals=0,
        ),
    )(inner, down, after)


def pack_kernel(terms, *refs):
    outs = refs[2 * terms :]
    for half in range(2):
        total = refs[half * terms][...].astype(jnp.float32)
        for i in range(1, terms):
            total = total + refs[half * terms + i][...].astype(jnp.float32)
        total = total.astype(jnp.bfloat16)
        for d in range(SIDE):
            outs[d][half * 16 : half * 16 + 16, :] = total[d * 16 : (d + 1) * 16]


def packed_sums(own, other):
    terms, width = len(own), own[0].shape[1]
    return pl.pallas_call(
        lambda *refs: pack_kernel(terms, *refs),
        in_specs=whole(*("v" * 2 * terms)),
        out_specs=whole(*("v" * SIDE)),
        out_shape=[jax.ShapeDtypeStruct((32, width), jnp.bfloat16)] * SIDE,
        compiler_params=pltpu.CompilerParams(vmem_limit_bytes=12582912),
    )(*own, *other)


def pick_kernel(at_ref, where, *refs):
    shards, outs = refs[: 2 * SIDE], refs[-2:]
    for half in range(2):
        for i in range(SIDE):
            for k in range(SIDE):
                columns = pl.ds(pl.multiple_of(at_ref[i * 2 * SIDE + half * SIDE + k] * 256, 256), 256)
                shard = shards[half * SIDE + i]
                outs[half][:, columns] = shard[k, where[half] * SIDE + where[1 - half]]


def pick_hidden(at, where, shards, after):
    shards = [r.reshape(SIDE, 16, 16, r.shape[-1]) for r in shards]
    return pl.pallas_call(
        pick_kernel,
        in_specs=whole("s", "s", *("v" * len(shards))) + [pl.BlockSpec(memory_space=pl.ANY)],
        out_specs=whole(*"vv"),
        out_shape=[jax.ShapeDtypeStruct((16, 16 * shards[0].shape[-1]), jnp.bfloat16)] * 2,
        compiler_params=pltpu.CompilerParams(vmem_limit_bytes=8 * 1024 * 1024),
    )(at, where, *shards, after)


def per_device(
    queries,
    key_rows,
    values,
    span_order,
    residual,
    out_weight,
    norm_gain,
    routes,
    route_gates,
    gate_proj,
    up_proj,
    down_proj,
):
    n_ctx = lax.axis_size("ctx")
    n_exp = lax.axis_size("exp")
    here = lax.axis_index("ctx")
    column = lax.axis_index("exp")
    core = column % 2
    z_here = column // 2
    block_rows = queries.shape[0]
    group = HEADS // KV_HEADS
    kv_local = key_rows.shape[1] // HD
    width = kv_local * HD
    token_count, model = residual.shape
    offsets = jnp.arange(block_rows, dtype=jnp.int32)
    back_places = (here - jnp.arange(CYCLE_STEPS, dtype=jnp.int32)) % n_ctx
    picked_place = back_places[:, None] == jnp.arange(n_ctx, dtype=jnp.int32)[None, :]
    starts = jnp.sum(jnp.where(picked_place, span_order[None, :], 0), axis=1) * block_rows
    key_pos = (starts[:, None] + offsets[None, :]).reshape(-1)
    query_pos = jnp.sum(jnp.where(picked_place[0], span_order, 0)) * block_rows + offsets

    packed = jnp.pad(key_rows, ((0, 0), (0, width))) + jnp.pad(values, ((0, 0), (width, 0)))

    def onward(shard, step):
        return lax.ppermute(shard, "ctx", [(i, (i + step) % n_ctx) for i in range(n_ctx)])

    collected = [packed] + [onward(packed, step) for step in range(1, CYCLE_STEPS)]
    flat_routes = routes.reshape(-1)
    pair_ids = jnp.arange(flat_routes.shape[0], dtype=jnp.int32)
    same_expert = flat_routes[:, None] == flat_routes[None, :]
    earlier = pair_ids[None, :] < pair_ids[:, None]
    slot_number = jnp.sum(jnp.where(same_expert & earlier, 1, 0), axis=1).astype(jnp.int32)
    other_core = (flat_routes + core) % 2
    codes = ((flat_routes // 2 * 2 + other_core) * CAP + slot_number).astype(jnp.bfloat16)
    codes = jnp.pad(codes.reshape(token_count, 2), ((0, 0), (0, HD - 2)))
    z_places = jnp.arange(SIDE, dtype=jnp.int32)
    columns = out_weight.shape[1]
    by_column = jnp.moveaxis(residual.reshape(token_count, n_ctx, columns), 1, 0)
    by_column = jnp.concatenate(
        [by_column, jnp.broadcast_to(codes[None], (n_ctx, token_count, HD))], axis=2
    )
    weight_other = sibling(out_weight)
    stacked = jnp.concatenate(collected, axis=0)
    key_all = stacked[:, :width].reshape(-1, kv_local, HD)
    value_all = stacked[:, width:].reshape(-1, kv_local, HD)
    query_heads = queries.reshape(block_rows, kv_local, group, HD)
    scores = jnp.einsum(
        "qkgd,lkd->kgql", query_heads, key_all, preferred_element_type=jnp.float32
    ) * (1.0 / math.sqrt(HD))
    admitted = key_pos[None, :] <= query_pos[:, None]
    scores = jnp.where(admitted[None, None], scores, -1e30)
    row_max = jnp.max(scores, axis=-1, keepdims=True)
    exp_scores = jnp.exp(scores - row_max)
    attend_probs = (exp_scores / jnp.sum(exp_scores, axis=-1, keepdims=True)).astype(jnp.bfloat16)
    mixed = jnp.einsum(
        "kgql,lkd->qkgd", attend_probs, value_all, preferred_element_type=jnp.float32
    )
    attended = mixed.astype(jnp.bfloat16).reshape(SIDE, 2, token_count, kv_local * group * HD)

    half = SIDE * token_count
    rows_0 = attended[:, 0].reshape(half, -1)
    rows_1 = attended[:, 1].reshape(half, -1)
    kept = jnp.where(core == 0, rows_0, rows_1)
    given = jnp.where(core == 0, rows_1, rows_0)
    paired = jnp.concatenate([kept, sibling(given)], axis=1)
    line = gathered(paired, first_axis)
    by_column, line[1] = lax.optimization_barrier((by_column, line[1]))
    by_column = lax.all_to_all(by_column, "ctx", split_axis=0, concat_axis=0, tiled=True)
    residual_slab = by_column[:, :, :columns]
    codes = by_column[None, :, :, columns:]
    codes = jnp.concatenate([codes, lax.ppermute(codes, BOTH, z_exchange(1))], axis=0)
    codes = jnp.concatenate([codes, lax.ppermute(codes, BOTH, z_exchange(2))], axis=0)
    line = jnp.concatenate(line, axis=0)
    plane = gathered(line, second_axis)

    x_here, y_here = here // SIDE, here % SIDE
    second = jnp.where(core == 0, x_here, y_here)
    first = jnp.where(core == 0, y_here, x_here)
    where = jnp.stack([second, first, z_here]).astype(jnp.int32)
    k2, k1 = z_places[:, None], z_places[None, :]
    by_x = ((x_here - k2) % SIDE * SIDE + (y_here - k1) % SIDE).astype(jnp.int32)
    by_y = ((x_here - k1) % SIDE * SIDE + (y_here - k2) % SIDE).astype(jnp.int32)
    place = jnp.where(core == 0, by_x, by_y)
    place_other = jnp.where(core == 0, by_y, by_x)
    spread = project(
        where, place.reshape(-1), plane, out_weight, weight_other, residual_slab, codes
    )

    rows = added(dealt([spread[d] for d in range(SIDE)], z_axis, 1)).astype(jnp.bfloat16)
    rows = rows.reshape(2, SIDE * SIDE * SIDE * CAP, columns)
    line = gathered(rows, first_axis)
    own = jnp.stack([r[0] for r in line])
    other = jnp.stack([r[1] for r in line])
    mine, theirs = {0: own}, {0: sibling(other)}
    for d in (1, -1):
        mine[d] = lax.ppermute(own, BOTH, second_axis(d))
        theirs[d] = lax.ppermute(other, BOTH, crossed(d))
    gain = norm_gain.astype(jnp.float32).reshape(n_ctx, 1, columns)
    gate_w, up_w, down_w = gate_proj[0], up_proj[0], down_proj[0]

    def at(*shifts):
        return jnp.concatenate([place[d] for d in shifts] + [place_other[d] for d in shifts])

    near = first_products(at(0), [mine[0]], [theirs[0]], gain, gate_w, up_w)
    on_mine, on_theirs, *near = lax.optimization_barrier((mine[1], theirs[-1], *near))
    mine[2] = lax.ppermute(on_mine, BOTH, second_axis(1))
    theirs[2] = lax.ppermute(on_theirs, BOTH, first_axis(-1))
    sides = first_products(
        at(1, 3), [mine[1], mine[-1]], [theirs[1], theirs[-1]], gain, gate_w, up_w, tuple(near)
    )
    far_mine, far_theirs, inner = last_products(
        at(2), mine[2], theirs[2], gain, gate_w, up_w, tuple(sides), down_w, where
    )
    side_out = down_products((1, 3), inner, down_w, far_mine)
    far_mine = lax.ppermute(far_mine, BOTH, second_axis(-1))
    far_theirs = lax.ppermute(far_theirs, BOTH, first_axis(1))
    near_out = down_products((0,), inner, down_w, far_theirs)
    back_mine, back_theirs, front_mine, front_theirs = side_out
    own = [near_out[0], lax.ppermute(front_mine, BOTH, second_axis(1))]
    other = [sibling(near_out[1]), lax.ppermute(back_theirs, BOTH, uncrossed(1))]
    back_mine = added([back_mine, far_mine]).astype(jnp.bfloat16)
    front_theirs = added([front_theirs, far_theirs]).astype(jnp.bfloat16)
    own.append(lax.ppermute(back_mine, BOTH, second_axis(-1)))
    other.append(lax.ppermute(front_theirs, BOTH, uncrossed(-1)))
    line = packed_sums(own, other)
    n1 = SIDE * CAP

    names = (0, 1, -1, 2)
    hidden_mine, hidden_theirs = pick_hidden(
        jnp.concatenate([at(0), at(1), at(3), at(2)]),
        where,
        [mine[d] for d in names] + [theirs[d] for d in names],
        side_out[0],
    )
    hidden_rows = jnp.concatenate([hidden_mine, sibling(hidden_theirs)], axis=0)
    slots = n_exp * CAP
    ahead = (flat_routes // 2 - z_here) % SIDE
    target = (ahead * 2 + other_core) * CAP + slot_number
    match_table = jnp.where(
        target[:, None] == jnp.arange(slots, dtype=jnp.int32)[None, :], 1.0, 0.0
    ).astype(jnp.bfloat16)
    per_z = 2 * CAP
    column_rows = added(dealt(line, first_axis, -1)).astype(jnp.bfloat16)
    row = jnp.arange(slots, dtype=jnp.int32)
    source = (row // CAP % 2) * n1 + (z_here - row // per_z) % SIDE * CAP + row % CAP
    reorder = jnp.where(source[:, None] == row[None, :], 1.0, 0.0).astype(jnp.bfloat16)
    column_rows = jnp.concatenate([column_rows, hidden_rows], axis=1)
    sent = jnp.dot(reorder, column_rows, preferred_element_type=jnp.float32).astype(jnp.bfloat16)
    sent = [sent[d * per_z : (d + 1) * per_z] for d in range(SIDE)]
    expert_rows = jnp.concatenate(dealt(sent, z_axis, -1), axis=0)
    picked = jnp.dot(match_table, expert_rows, preferred_element_type=jnp.float32).reshape(
        token_count, 2, -1
    )
    total = (
        picked[:, 0, model:]
        + route_gates[:, 0:1] * picked[:, 0, :model]
        + route_gates[:, 1:2] * picked[:, 1, :model]
    )
    return total.astype(jnp.bfloat16)


def solution(mesh):
    return jax.shard_map(
        per_device,
        mesh=mesh,
        in_specs=(
            P("ctx", "exp"),
            P("ctx", "exp"),
            P("ctx", "exp"),
            P(),
            P(("ctx", "exp"), None),
            P("exp", "ctx"),
            P(),
            P(("ctx", "exp"), None),
            P(("ctx", "exp"), None),
            P("exp", None, "ctx"),
            P("exp", None, "ctx"),
            P("exp", "ctx", None),
        ),
        out_specs=P(("ctx", "exp"), None),
        check_vma=False,
    )
```

```python
import math

import jax
import jax.numpy as jnp
from jax import lax
from jax.experimental import pallas as pl
from jax.experimental.pallas import tpu as pltpu
from jax.sharding import PartitionSpec as P

HEADS = 64
KV_HEADS = 8
HD = 128
CYCLE_STEPS = 4
CAP = 4
SIDE = 4
BOTH = ("ctx", "exp")
SHIFTS = (1, 3, 2)


def number(x, y, z, core):
    return (((x % SIDE) * SIDE + y % SIDE) * SIDE + z % SIDE) * 2 + core


def everyone():
    return [
        (x, y, z, core)
        for x in range(SIDE)
        for y in range(SIDE)
        for z in range(SIDE)
        for core in range(2)
    ]


def first_axis(d):
    return [
        (number(x, y, z, c), number(x + d * c, y + d * (1 - c), z, c)) for x, y, z, c in everyone()
    ]


def second_axis(d):
    return [
        (number(x, y, z, c), number(x + d * (1 - c), y + d * c, z, c)) for x, y, z, c in everyone()
    ]


def crossed(d):
    return [
        (number(x, y, z, c), number(x + d * (1 - c), y + d * c, z, 1 - c)) for x, y, z, c in everyone()
    ]


def uncrossed(d):
    return [(to, start) for start, to in crossed(d)]


def z_axis(d):
    return [(number(x, y, z, c), number(x, y, z + d, c)) for x, y, z, c in everyone()]


def z_exchange(bit):
    return [(number(x, y, z, c), number(x, y, z ^ bit, c)) for x, y, z, c in everyone()]


def sibling(shard):
    pairs = [(number(x, y, z, c), number(x, y, z, 1 - c)) for x, y, z, c in everyone()]
    return lax.ppermute(shard, BOTH, pairs)


def gathered(shard, along):
    got = {0: shard}
    for d in SHIFTS:
        got[d] = lax.ppermute(shard, BOTH, along(d))
    return [got[d] for d in range(SIDE)]


def dealt(blocks, along, sign):
    got = {0: blocks[0]}
    for d in SHIFTS:
        got[d] = lax.ppermute(blocks[d], BOTH, along(sign * d))
    return [got[d] for d in range(SIDE)]


def added(blocks):
    total = blocks[0].astype(jnp.float32)
    for block in blocks[1:]:
        total = total + block.astype(jnp.float32)
    return total


def whole(*names):
    spaces = {"v": pltpu.VMEM, "s": pltpu.SMEM}
    return [pl.BlockSpec(memory_space=spaces[n]) for n in names]


def project_kernel(where, place, p0, p1, p2, p3, w0, w1, res, codes_ref, spread, wide, named_by):
    depth = w0.shape[0]
    for k2, piece in enumerate((p0, p1, p2, p3)):
        part = jnp.dot(piece[:, :depth], w0[...], preferred_element_type=jnp.float32)
        part += jnp.dot(piece[:, depth : 2 * depth], w1[...], preferred_element_type=jnp.float32)
        for k1 in range(SIDE):
            at = place[k2 * SIDE + k1]
            residual = res[at].astype(jnp.float32)
            for zt in range(SIDE):
                lo = (k1 * SIDE + zt) * 8
                seg = part[lo : lo + 8]
                named_by[lo : lo + 8] = codes_ref[zt ^ where[2], at].astype(jnp.float32)
                wide[lo : lo + 8] = seg + jnp.where(zt == where[2], residual, 0.0)
        rows = wide[...].astype(jnp.bfloat16)
        codes = named_by[...]
        shape = (rows.shape[0], 16 * 2 * SIDE * CAP)
        slot = lax.broadcasted_iota(jnp.int32, shape, 1)
        group = lax.broadcasted_iota(jnp.int32, shape, 0) // 8
        code = ((slot // 64) * CAP + slot % CAP).astype(jnp.float32)
        named = jnp.logical_or(codes[:, 0:1] == code, codes[:, 1:2] == code)
        hit = jnp.logical_and(named, (slot % 64) // CAP == group)
        table = jnp.where(hit, 1.0, 0.0).astype(jnp.bfloat16)
        chosen = lax.dot_general(
            table, rows, (((0,), (0,)), ((), ())), preferred_element_type=jnp.float32
        ).astype(spread.dtype)
        i2 = (where[0] - k2 + SIDE) % SIDE
        for zt in range(SIDE):
            ahead = (zt - where[2] + SIDE) % SIDE
            for p in range(2):
                for k1 in range(SIDE):
                    lo = (zt * 2 + p) * 64 + k1 * 16
                    spread[ahead, p, i2, (where[1] - k1 + SIDE) % SIDE] = chosen[lo : lo + 16]


def project(where, place, pieces, w0, w1, res, codes):
    columns = w0.shape[1]
    return pl.pallas_call(
        project_kernel,
        in_specs=whole(*"ssvvvvvvvv"),
        out_specs=whole("v")[0],
        out_shape=jax.ShapeDtypeStruct((SIDE, 2, SIDE, SIDE, 4 * CAP, columns), jnp.bfloat16),
        scratch_shapes=[
            pltpu.VMEM((pieces[0].shape[0], columns), jnp.float32),
            pltpu.VMEM((pieces[0].shape[0], HD), jnp.float32),
        ],
        compiler_params=pltpu.CompilerParams(vmem_limit_bytes=10485760),
        cost_estimate=pl.CostEstimate(
            flops=2 * 512 * 2048 * 256 + 2 * 2048 * 128 * 256,
            bytes_accessed=6 * 1024 * 1024,
            transcendentals=0,
        ),
    )(where, place, *pieces, w0, w1, res, codes)


def hidden_step(blocks, at, row, gate_ref, up_ref, gain_ref, gate_in, up_in, sq_in, outs):
    gate_out, up_out, sq_out = outs
    rows = pl.ds(row, 256)
    gate = up = sq = None
    for block, c in zip(blocks, at):
        wide = block.astype(jnp.float32)
        square = wide * wide
        square = square[:, :128] + square[:, 128:]
        x = (wide * gain_ref[c]).astype(jnp.bfloat16)
        k = pl.ds(pl.multiple_of(c * 256, 256), 256)
        g = jnp.dot(x, gate_ref[k, :], preferred_element_type=jnp.float32)
        u = jnp.dot(x, up_ref[k, :], preferred_element_type=jnp.float32)
        gate = g if gate is None else gate + g
        up = u if up is None else up + u
        sq = square if sq is None else sq + square
    if gate_in is not None:
        gate, up, sq = gate + gate_in[rows], up + up_in[rows], sq + sq_in[rows]
    gate_out[rows], up_out[rows], sq_out[rows] = gate, up, sq


def first_kernel(count, has_sums, *refs):
    at_ref = refs[0]
    shards = refs[1 : 1 + 2 * count]
    gain_ref, gate_ref, up_ref = refs[1 + 2 * count : 4 + 2 * count]
    sums = refs[4 + 2 * count : 7 + 2 * count] if has_sums else (None, None, None)
    outs = refs[-3:]
    for half in range(2):
        blocks = [shards[half * count + i][k] for i in range(count) for k in range(SIDE)]
        at = [at_ref[(half * count + i) * SIDE + k] for i in range(count) for k in range(SIDE)]
        hidden_step(blocks, at, half * 256, gate_ref, up_ref, gain_ref, *sums, outs)


def first_products(at, mine, theirs, gain, gate, up, sums=()):
    count = len(mine)
    hidden = gate.shape[1]
    wide = jax.ShapeDtypeStruct((512, hidden), jnp.float32)
    return pl.pallas_call(
        lambda *refs: first_kernel(count, bool(sums), *refs),
        in_specs=whole("s", *("v" * (2 * count + 3 + len(sums)))),
        out_specs=whole(*"vvv"),
        out_shape=[wide, wide, jax.ShapeDtypeStruct((512, 128), jnp.float32)],
        input_output_aliases={4 + 2 * count + i: i for i in range(len(sums))},
        compiler_params=pltpu.CompilerParams(vmem_limit_bytes=10485760),
        cost_estimate=pl.CostEstimate(
            flops=4 * 512 * 1024 * count * hidden,
            bytes_accessed=4096 * count * hidden,
            transcendentals=0,
        ),
    )(at, *mine, *theirs, gain, gate, up, *sums)


def last_kernel(width, at_ref, mine, theirs, gain, gate_w, up_w, gate_in, up_in, sq_in, down, where, *refs):
    out_mine, out_theirs, rest, gate, up, sq, inner = refs
    for half, shard in enumerate((mine, theirs)):
        blocks = [shard[k] for k in range(SIDE)]
        at = [at_ref[half * SIDE + k] for k in range(SIDE)]
        hidden_step(blocks, at, half * 256, gate_w, up_w, gain, gate_in, up_in, sq_in, (gate, up, sq))
    for half in range(2):
        rows = pl.ds(half * 256, 256)
        mean = jnp.sum(sq[rows], axis=1, keepdims=True) * (1.0 / width)
        scale = lax.rsqrt(mean + 1e-06)
        g = gate[rows] * scale
        u = up[rows] * scale
        act = (g / (1.0 + jnp.exp(-g)) * u).astype(jnp.bfloat16)
        for i in range(16):
            inner[half * 16 + i] = act[i * 16 : (i + 1) * 16]
    for half in range(2):
        for d in range(SIDE):
            i2 = (where[half] - d + SIDE) % SIDE
            for j in range(SIDE):
                i1 = (where[1 - half] - j + SIDE) % SIDE
                rest[((d * 2 + half) * SIDE + j) * 16 : ((d * 2 + half) * SIDE + j + 1) * 16, :] = inner[
                    half * 16 + i2 * SIDE + i1
                ]
    part = jnp.dot(rest[256:384, :], down[...], preferred_element_type=jnp.float32)
    part = part.astype(jnp.bfloat16)
    out_mine[...] = part[:64]
    out_theirs[...] = part[64:]


def last_products(at, mine, theirs, gain, gate, up, sums, down, where):
    hidden, width = down.shape
    return pl.pallas_call(
        lambda *refs: last_kernel(width, *refs),
        in_specs=whole(*"svvvvvvvvvs"),
        out_specs=whole(*"vvv"),
        out_shape=[jax.ShapeDtypeStruct((64, width), jnp.bfloat16)] * 2
        + [jax.ShapeDtypeStruct((512, hidden), jnp.bfloat16)],
        scratch_shapes=[
            pltpu.VMEM((512, hidden), jnp.float32),
            pltpu.VMEM((512, hidden), jnp.float32),
            pltpu.VMEM((512, 128), jnp.float32),
            pltpu.VMEM((32, 16, hidden), jnp.bfloat16),
        ],
        compiler_params=pltpu.CompilerParams(vmem_limit_bytes=12582912),
        cost_estimate=pl.CostEstimate(
            flops=4 * 512 * 1024 * hidden + 2 * 128 * hidden * width,
            bytes_accessed=4096 * hidden + 2 * hidden * width,
            transcendentals=512 * hidden,
        ),
    )(at, mine, theirs, gain, gate, up, *sums, down, where)


def down_kernel(picks, inner, down, after, *outs):
    for i, d in enumerate(picks):
        part = jnp.dot(
            inner[d * 128 : (d + 1) * 128, :], down[...], preferred_element_type=jnp.float32
        ).astype(jnp.bfloat16)
        outs[2 * i][...] = part[:64]
        outs[2 * i + 1][...] = part[64:]


def down_products(picks, inner, down, after):
    hidden, width = down.shape
    return pl.pallas_call(
        lambda *refs: down_kernel(picks, *refs),
        in_specs=whole(*"vv") + [pl.BlockSpec(memory_space=pl.ANY)],
        out_specs=whole(*("vv" * len(picks))),
        out_shape=[jax.ShapeDtypeStruct((64, width), jnp.bfloat16)] * (2 * len(picks)),
        compiler_params=pltpu.CompilerParams(vmem_limit_bytes=8388608),
        cost_estimate=pl.CostEstimate(
            flops=2 * 128 * len(picks) * hidden * width,
            bytes_accessed=2 * hidden * width,
            transcendentals=0,
        ),
    )(inner, down, after)


def pack_kernel(terms, *refs):
    outs = refs[2 * terms :]
    for half in range(2):
        total = refs[half * terms][...].astype(jnp.float32)
        for i in range(1, terms):
            total = total + refs[half * terms + i][...].astype(jnp.float32)
        total = total.astype(jnp.bfloat16)
        for d in range(SIDE):
            outs[d][half * 16 : half * 16 + 16, :] = total[d * 16 : (d + 1) * 16]


def packed_sums(own, other):
    terms, width = len(own), own[0].shape[1]
    return pl.pallas_call(
        lambda *refs: pack_kernel(terms, *refs),
        in_specs=whole(*("v" * 2 * terms)),
        out_specs=whole(*("v" * SIDE)),
        out_shape=[jax.ShapeDtypeStruct((32, width), jnp.bfloat16)] * SIDE,
        compiler_params=pltpu.CompilerParams(vmem_limit_bytes=6291456),
    )(*own, *other)


def unpack_kernel(has_hidden, a, b, c, d, order, *refs):
    total = a[...].astype(jnp.float32)
    for shard in (b, c, d):
        total = total + shard[...].astype(jnp.float32)
    table = order[...]
    rows = jnp.dot(table, total.astype(jnp.bfloat16), preferred_element_type=jnp.float32)
    width = a.shape[1]
    outs = refs[1:] if has_hidden else refs
    for i, out in enumerate(outs):
        out[:, :width] = rows[i * 8 : (i + 1) * 8].astype(out.dtype)
    if has_hidden:
        rows = jnp.dot(table, refs[0][...], preferred_element_type=jnp.float32)
        for i, out in enumerate(outs):
            out[:, width:] = rows[i * 8 : (i + 1) * 8].astype(out.dtype)


def unpacked(blocks, order, hidden=None):
    width = blocks[0].shape[1]
    more = [] if hidden is None else [hidden]
    return pl.pallas_call(
        lambda *refs: unpack_kernel(bool(more), *refs),
        in_specs=whole(*("v" * (5 + len(more)))),
        out_specs=whole(*("v" * SIDE)),
        out_shape=[jax.ShapeDtypeStruct((8, width * (1 + len(more))), jnp.bfloat16)] * SIDE,
        compiler_params=pltpu.CompilerParams(vmem_limit_bytes=5242880),
    )(*blocks, order, *more)


def pick_kernel(at_ref, where, *refs):
    shards, outs = refs[: 2 * SIDE], refs[-2:]
    for half in range(2):
        for i in range(SIDE):
            for k in range(SIDE):
                columns = pl.ds(pl.multiple_of(at_ref[i * 2 * SIDE + half * SIDE + k] * 256, 256), 256)
                shard = shards[half * SIDE + i]
                outs[half][:, columns] = shard[k, where[half] * SIDE + where[1 - half]]


def pick_hidden(at, where, shards, after):
    shards = [r.reshape(SIDE, 16, 16, r.shape[-1]) for r in shards]
    return pl.pallas_call(
        pick_kernel,
        in_specs=whole("s", "s", *("v" * len(shards))) + [pl.BlockSpec(memory_space=pl.ANY)],
        out_specs=whole(*"vv"),
        out_shape=[jax.ShapeDtypeStruct((16, 16 * shards[0].shape[-1]), jnp.bfloat16)] * 2,
        compiler_params=pltpu.CompilerParams(vmem_limit_bytes=4194304),
    )(at, where, *shards, after)


def per_device(
    queries,
    key_rows,
    values,
    span_order,
    residual,
    out_weight,
    norm_gain,
    routes,
    route_gates,
    gate_proj,
    up_proj,
    down_proj,
):
    n_ctx = lax.axis_size("ctx")
    n_exp = lax.axis_size("exp")
    here = lax.axis_index("ctx")
    column = lax.axis_index("exp")
    core = column % 2
    z_here = column // 2
    block_rows = queries.shape[0]
    group = HEADS // KV_HEADS
    kv_local = key_rows.shape[1] // HD
    width = kv_local * HD
    token_count, model = residual.shape
    offsets = jnp.arange(block_rows, dtype=jnp.int32)
    back_places = (here - jnp.arange(CYCLE_STEPS, dtype=jnp.int32)) % n_ctx
    picked_place = back_places[:, None] == jnp.arange(n_ctx, dtype=jnp.int32)[None, :]
    starts = jnp.sum(jnp.where(picked_place, span_order[None, :], 0), axis=1) * block_rows
    key_pos = (starts[:, None] + offsets[None, :]).reshape(-1)
    query_pos = jnp.sum(jnp.where(picked_place[0], span_order, 0)) * block_rows + offsets

    packed = jnp.pad(key_rows, ((0, 0), (0, width))) + jnp.pad(values, ((0, 0), (width, 0)))

    def onward(shard, step):
        return lax.ppermute(shard, "ctx", [(i, (i + step) % n_ctx) for i in range(n_ctx)])

    collected = [packed] + [onward(packed, step) for step in range(1, CYCLE_STEPS)]
    flat_routes = routes.reshape(-1)
    pair_ids = jnp.arange(flat_routes.shape[0], dtype=jnp.int32)
    same_expert = flat_routes[:, None] == flat_routes[None, :]
    earlier = pair_ids[None, :] < pair_ids[:, None]
    slot_number = jnp.sum(jnp.where(same_expert & earlier, 1, 0), axis=1).astype(jnp.int32)
    other_core = (flat_routes + core) % 2
    codes = ((flat_routes // 2 * 2 + other_core) * CAP + slot_number).astype(jnp.bfloat16)
    codes = jnp.pad(codes.reshape(token_count, 2), ((0, 0), (0, HD - 2)))
    z_places = jnp.arange(SIDE, dtype=jnp.int32)
    columns = out_weight.shape[1]
    by_column = jnp.moveaxis(residual.reshape(token_count, n_ctx, columns), 1, 0)
    by_column = jnp.concatenate(
        [by_column, jnp.broadcast_to(codes[None], (n_ctx, token_count, HD))], axis=2
    )
    weight_other = sibling(out_weight)
    stacked = jnp.concatenate(collected, axis=0)
    key_all = stacked[:, :width].reshape(-1, kv_local, HD)
    value_all = stacked[:, width:].reshape(-1, kv_local, HD)
    query_heads = queries.reshape(block_rows, kv_local, group, HD)
    scores = jnp.einsum(
        "qkgd,lkd->kgql", query_heads, key_all, preferred_element_type=jnp.float32
    ) * (1.0 / math.sqrt(HD))
    admitted = key_pos[None, :] <= query_pos[:, None]
    scores = jnp.where(admitted[None, None], scores, -1e30)
    row_max = jnp.max(scores, axis=-1, keepdims=True)
    exp_scores = jnp.exp(scores - row_max)
    attend_probs = (exp_scores / jnp.sum(exp_scores, axis=-1, keepdims=True)).astype(jnp.bfloat16)
    mixed = jnp.einsum(
        "kgql,lkd->qkgd", attend_probs, value_all, preferred_element_type=jnp.float32
    )
    attended = mixed.astype(jnp.bfloat16).reshape(SIDE, 2, token_count, kv_local * group * HD)

    half = SIDE * token_count
    rows_0 = attended[:, 0].reshape(half, -1)
    rows_1 = attended[:, 1].reshape(half, -1)
    kept = jnp.where(core == 0, rows_0, rows_1)
    given = jnp.where(core == 0, rows_1, rows_0)
    paired = jnp.concatenate([kept, sibling(given)], axis=1)
    line = gathered(paired, first_axis)
    by_column, line[1] = lax.optimization_barrier((by_column, line[1]))
    by_column = lax.all_to_all(by_column, "ctx", split_axis=0, concat_axis=0, tiled=True)
    residual_slab = by_column[:, :, :columns]
    codes = by_column[None, :, :, columns:]
    codes = jnp.concatenate([codes, lax.ppermute(codes, BOTH, z_exchange(1))], axis=0)
    codes = jnp.concatenate([codes, lax.ppermute(codes, BOTH, z_exchange(2))], axis=0)
    line = jnp.concatenate(line, axis=0)
    plane = gathered(line, second_axis)

    x_here, y_here = here // SIDE, here % SIDE
    second = jnp.where(core == 0, x_here, y_here)
    first = jnp.where(core == 0, y_here, x_here)
    where = jnp.stack([second, first, z_here]).astype(jnp.int32)
    k2, k1 = z_places[:, None], z_places[None, :]
    by_x = ((x_here - k2) % SIDE * SIDE + (y_here - k1) % SIDE).astype(jnp.int32)
    by_y = ((x_here - k1) % SIDE * SIDE + (y_here - k2) % SIDE).astype(jnp.int32)
    place = jnp.where(core == 0, by_x, by_y)
    place_other = jnp.where(core == 0, by_y, by_x)
    spread = project(
        where, place.reshape(-1), plane, out_weight, weight_other, residual_slab, codes
    )

    rows = added(dealt([spread[d] for d in range(SIDE)], z_axis, 1)).astype(jnp.bfloat16)
    rows = rows.reshape(2, SIDE * SIDE * SIDE * CAP, columns)
    line = gathered(rows, first_axis)
    own = jnp.stack([r[0] for r in line])
    other = jnp.stack([r[1] for r in line])
    mine, theirs = {0: own}, {0: sibling(other)}
    for d in (1, -1):
        mine[d] = lax.ppermute(own, BOTH, second_axis(d))
        theirs[d] = lax.ppermute(other, BOTH, crossed(d))
    gain = norm_gain.astype(jnp.float32).reshape(n_ctx, 1, columns)
    gate_w, up_w, down_w = gate_proj[0], up_proj[0], down_proj[0]

    def at(*shifts):
        return jnp.concatenate([place[d] for d in shifts] + [place_other[d] for d in shifts])

    near = first_products(at(0), [mine[0]], [theirs[0]], gain, gate_w, up_w)
    on_mine, on_theirs, *near = lax.optimization_barrier((mine[1], theirs[-1], *near))
    mine[2] = lax.ppermute(on_mine, BOTH, second_axis(1))
    theirs[2] = lax.ppermute(on_theirs, BOTH, first_axis(-1))
    sides = first_products(
        at(1, 3), [mine[1], mine[-1]], [theirs[1], theirs[-1]], gain, gate_w, up_w, tuple(near)
    )
    far_mine, far_theirs, inner = last_products(
        at(2), mine[2], theirs[2], gain, gate_w, up_w, tuple(sides), down_w, where
    )
    side_out = down_products((1, 3), inner, down_w, far_mine)
    far_mine = lax.ppermute(far_mine, BOTH, second_axis(-1))
    far_theirs = lax.ppermute(far_theirs, BOTH, first_axis(1))
    near_out = down_products((0,), inner, down_w, far_theirs)
    back_mine, back_theirs, front_mine, front_theirs = side_out
    own = [near_out[0], lax.ppermute(front_mine, BOTH, second_axis(1))]
    other = [sibling(near_out[1]), lax.ppermute(back_theirs, BOTH, uncrossed(1))]
    back_mine = added([back_mine, far_mine]).astype(jnp.bfloat16)
    front_theirs = added([front_theirs, far_theirs]).astype(jnp.bfloat16)
    own.append(lax.ppermute(back_mine, BOTH, second_axis(-1)))
    other.append(lax.ppermute(front_theirs, BOTH, uncrossed(-1)))
    line = packed_sums(own, other)
    n1 = SIDE * CAP

    names = (0, 1, -1, 2)
    hidden_mine, hidden_theirs = pick_hidden(
        jnp.concatenate([at(0), at(1), at(3), at(2)]),
        where,
        [mine[d] for d in names] + [theirs[d] for d in names],
        near_out[0],
    )
    hidden_rows = jnp.concatenate([hidden_mine, sibling(hidden_theirs)], axis=0)
    slots = n_exp * CAP
    ahead = (flat_routes // 2 - z_here) % SIDE
    target = (ahead * 2 + other_core) * CAP + slot_number
    match_table = jnp.where(
        target[:, None] == jnp.arange(slots, dtype=jnp.int32)[None, :], 1.0, 0.0
    ).astype(jnp.bfloat16)
    per_z = 2 * CAP
    row = jnp.arange(slots, dtype=jnp.int32)
    source = (row // CAP % 2) * n1 + (z_here - row // per_z) % SIDE * CAP + row % CAP
    reorder = jnp.where(source[:, None] == row[None, :], 1.0, 0.0).astype(jnp.bfloat16)
    sent = unpacked(dealt(line, first_axis, -1), reorder, hidden_rows)
    expert_rows = jnp.concatenate(dealt(sent, z_axis, -1), axis=0)
    picked = jnp.dot(match_table, expert_rows, preferred_element_type=jnp.float32).reshape(
        token_count, 2, -1
    )
    total = (
        picked[:, 0, model:]
        + route_gates[:, 0:1] * picked[:, 0, :model]
        + route_gates[:, 1:2] * picked[:, 1, :model]
    )
    return total.astype(jnp.bfloat16)


def solution(mesh):
    return jax.shard_map(
        per_device,
        mesh=mesh,
        in_specs=(
            P("ctx", "exp"),
            P("ctx", "exp"),
            P("ctx", "exp"),
            P(),
            P(("ctx", "exp"), None),
            P("exp", "ctx"),
            P(),
            P(("ctx", "exp"), None),
            P(("ctx", "exp"), None),
            P("exp", None, "ctx"),
            P("exp", None, "ctx"),
            P("exp", "ctx", None),
        ),
        out_specs=P(("ctx", "exp"), None),
        check_vma=False,
    )
```
